128 devices in a mesh: dp: 4 (over z), proto: 32 (over y, x, core).
Axes of the slice: x: 4, y: 4, z: 4, core: 2. Of those that a mesh axis runs over, the one named last changes fastest.
Arguments:
- teacher_hidden: bfloat16 [3072, 2048], P(('dp', 'proto')), may hold values from -6 to 6
- teacher_proj: bfloat16 [2048, 384], replicated, may hold values from -5.524272 to 5.524272
- student_hidden: bfloat16 [3072, 384], P(('dp', 'proto')), may hold values from -8 to 8
- teacher_protos: bfloat16 [384, 131072], P(None, ('dp', 'proto')), may hold values from -8 to 8
- student_protos: bfloat16 [384, 131072], P(None, ('dp', 'proto')), may hold values from -8 to 8
Outputs:
- loss_mean: float32 [], replicated
- d_student: float32 [3072, 384], P(('dp', 'proto'))
- d_protos: float32 [384, 131072], P(None, ('dp', 'proto'))
The draws below stay inside these ranges and needn't reach their ends.
All inputs are finite; a program needn't handle non-finite values.
Results may differ from the reference program's by a relative error of at most 0.0021.
Values may be sent and summed in bfloat16 or wider, within the bound.
No kernel may reach another device: no remote copies, remote signals or barrier semaphores. Data moves between devices by JAX's collectives and lax.ppermute only.
A program may use at most 128 MiB of HBM per device.

```python
import jax
import jax.numpy as jnp
from jax import lax

HEAD = 2048
BOT = 384
K = 131072
ITERS = 3
IMAGES = 3072
N_DP = 4
N_PROTO = 32


def coord_profile(key):
    spread = jax.random.uniform(jax.random.fold_in(key, 101), (BOT,), jnp.float32)
    return jnp.exp(3.7 * spread ** 10)


def common_direction(key, profile):
    signs = jax.random.randint(jax.random.fold_in(key, 102), (BOT,), 0, 2).astype(jnp.float32)
    size = jnp.sqrt(jnp.sum(profile * profile))
    return (2.0 * signs - 1.0) * BOT ** (-0.5) * size


def log_scales(key, count):
    spread = jax.random.uniform(key, (count,), jnp.float32)
    return jnp.exp(jnp.log(0.003) + spread * jnp.log(10.0))


def column_drift(strength):
    place = jnp.arange(K).astype(jnp.float32) / (K - 1.0)
    return strength * (1.0 - 2.0 * place)


def draw_teacher_proj(key, part):
    profile = coord_profile(key)
    direction = common_direction(key, profile)
    key = jax.random.fold_in(key, 1)
    base = jnp.clip(jax.random.normal(jax.random.fold_in(key, 7), (HEAD, BOT), jnp.float32), -6.0, 6.0)
    signs = jax.random.randint(jax.random.fold_in(key, 8), (HEAD,), 0, 2).astype(jnp.float32)
    along = (2.0 * signs - 1.0) * 0.5
    mixed = base * profile[None, :] + along[:, None] * direction[None, :]
    return (mixed * HEAD ** (-0.5)).astype(jnp.bfloat16)


def draw_student_hidden(key, part):
    profile = coord_profile(key)
    direction = common_direction(key, profile)
    key = jax.random.fold_in(key, 2)
    strength = 3.0
    base = jnp.clip(jax.random.normal(jax.random.fold_in(key, 7), (IMAGES, BOT), jnp.float32), -6.0, 6.0)
    rows = log_scales(jax.random.fold_in(key, 8), IMAGES)
    mixed = base * profile[None, :] + strength * direction[None, :]
    return (mixed * rows[:, None]).astype(jnp.bfloat16)


def draw_teacher_protos(key, part):
    profile = coord_profile(key)
    direction = common_direction(key, profile)
    key = jax.random.fold_in(key, 3)
    strength = 3.0
    base = jnp.clip(jax.random.normal(jax.random.fold_in(key, 7), (BOT, K), jnp.float32), -6.0, 6.0)
    cols = log_scales(jax.random.fold_in(key, 8), K)
    slope = column_drift(strength)
    mixed = base * profile[:, None] + direction[:, None] * slope[None, :]
    return (mixed * cols[None, :]).astype(jnp.bfloat16)


def draw_student_protos(key, part):
    profile = coord_profile(key)
    direction = common_direction(key, profile)
    key = jax.random.fold_in(key, 4)
    strength = 3.0
    base = jnp.clip(jax.random.normal(jax.random.fold_in(key, 7), (BOT, K), jnp.float32), -6.0, 6.0)
    cols = log_scales(jax.random.fold_in(key, 8), K)
    slope = column_drift(strength)
    mixed = base * profile[:, None] + direction[:, None] * slope[None, :]
    return (mixed * cols[None, :]).astype(jnp.bfloat16)


def steps_of(key, extent, split, low, top_value):
    loudness = 1.0
    for position, shards_of in split:
        steps = jax.random.uniform(jax.random.fold_in(jax.random.fold_in(key, 6), position), (shards_of,), jnp.float32, low / len(split), top_value / len(split))
        loudness = loudness * jnp.repeat(jnp.exp(steps), extent[position] // shards_of).reshape((-1,) + (1,) * (len(extent) - 1 - position))
    return loudness


def bell_draw(own_key, shape, scale, most, shards=(), kind=jnp.bfloat16):
    result = jax.random.normal(own_key, shape, jnp.float32) * scale
    if len(shards) > 0:
        result = steps_of(own_key, shape, shards, -0.22, 0.18) * result
    return jnp.clip(result, min=-most, max=most).astype(kind)


def setup_inputs(seed: int = 0) -> dict:
    key_list = jax.random.split(jax.random.key(seed), 6)
    return {
        "teacher_hidden": bell_draw(key_list[0], (IMAGES, HEAD), 1.0, 6.0, ((0, 128),)),
        "teacher_proj": draw_teacher_proj(jax.random.fold_in(key_list[5], 71), 0),
        "student_hidden": draw_student_hidden(jax.random.fold_in(key_list[5], 71), 0),
        "teacher_protos": draw_teacher_protos(jax.random.fold_in(key_list[5], 71), 0),
        "student_protos": draw_student_protos(jax.random.fold_in(key_list[5], 71), 0),
    }


EPS = 1e-06
teacher_temp = 0.07
student_temp = 0.1

def unit_columns(weights):
    widened = weights.astype(jnp.float32)
    inv_norm = lax.rsqrt(lax.optimization_barrier(jnp.sum(widened * widened, axis=0, keepdims=True)) + EPS)
    return (widened * inv_norm, inv_norm)

def reference(teacher_hidden, teacher_proj, student_hidden, teacher_protos, student_protos):
    t_hid = jnp.dot(teacher_hidden, teacher_proj, preferred_element_type=jnp.float32)
    t_bot = (t_hid * lax.rsqrt(lax.optimization_barrier(jnp.sum(t_hid * t_hid, axis=1, keepdims=True)) + EPS)).astype(jnp.bfloat16)
    s_hid = student_hidden.astype(jnp.float32)
    s_inv = lax.rsqrt(lax.optimization_barrier(jnp.sum(s_hid * s_hid, axis=1, keepdims=True)) + EPS)
    s_unit = s_hid * s_inv
    s_bot = s_unit.astype(jnp.bfloat16)
    blocks = N_DP * N_PROTO
    width = K // blocks
    t_blocks = teacher_protos.reshape(BOT, blocks, width).transpose(1, 0, 2)
    s_blocks = student_protos.reshape(BOT, blocks, width).transpose(1, 0, 2)

    def teacher_exp(block_w):
        unit_cols, _ = unit_columns(block_w)
        return jnp.exp(jnp.dot(t_bot, unit_cols.astype(jnp.bfloat16), preferred_element_type=jnp.float32) / teacher_temp)

    def student_logits(block_w):
        unit_cols, inv_norm = unit_columns(block_w)
        logits = jnp.dot(s_bot, unit_cols.astype(jnp.bfloat16), preferred_element_type=jnp.float32) / student_temp
        return (logits, unit_cols, inv_norm)

    def part_sum(carry_sum, block_w):
        logits, _, _ = student_logits(block_w)
        return (carry_sum + lax.optimization_barrier(jnp.sum(jnp.exp(logits), axis=1)), None)
    partition, _ = lax.scan(part_sum, jnp.zeros((IMAGES,), jnp.float32), s_blocks)
    log_total = jnp.log(partition)
    weight = jnp.ones((IMAGES,), jnp.float32)
    row_total = weight
    col_scales = jnp.zeros((blocks, width), jnp.float32)
    for sweep in range(ITERS):

        def sweep_block(carry_sum, block_w):
            exp_block = teacher_exp(block_w)
            col_scale = 1.0 / (K * lax.optimization_barrier(jnp.sum(exp_block * weight[:, None], axis=0)))
            return (carry_sum + lax.optimization_barrier(jnp.sum(exp_block * col_scale[None, :], axis=1)), col_scale)
        row_total, col_scales = lax.scan(sweep_block, jnp.zeros((IMAGES,), jnp.float32), t_blocks)
        weight = 1.0 / (IMAGES * row_total)

    def grad_block(carry, inputs):
        t_w, s_w, col_scale = inputs
        exp_block = teacher_exp(t_w)
        target = exp_block * col_scale[None, :] / row_total[:, None]
        logits, unit_cols, inv_norm = student_logits(s_w)
        loss_sum = carry[0] + jnp.sum(target * (log_total[:, None] - logits))
        grad_logits = ((jnp.exp(logits) / partition[:, None] - target) / student_temp).astype(jnp.bfloat16)
        d_unit = jnp.dot(s_bot.T, grad_logits, preferred_element_type=jnp.float32)
        d_block = inv_norm * (d_unit - unit_cols * lax.optimization_barrier(jnp.sum(unit_cols * d_unit, axis=0, keepdims=True)))
        d_bot = carry[1] + jnp.dot(grad_logits, unit_cols.astype(jnp.bfloat16).T, preferred_element_type=jnp.float32)
        return ((loss_sum, d_bot), d_block)
    start = (jnp.zeros((), jnp.float32), jnp.zeros((IMAGES, BOT), jnp.float32))
    (loss_sum, d_bot), d_blocks = lax.scan(grad_block, start, (t_blocks, s_blocks, col_scales))
    d_protos = d_blocks.transpose(1, 0, 2).reshape(BOT, K)
    d_student = s_inv * (d_bot - s_unit * lax.optimization_barrier(jnp.sum(s_unit * d_bot, axis=1, keepdims=True)))
    return (loss_sum / IMAGES, d_student, d_protos)
```

```python
import jax
import jax.numpy as jnp
from jax import lax
from jax.experimental import pallas as pl
from jax.experimental.pallas import tpu as pltpu
from jax.sharding import Mesh
from jax.sharding import PartitionSpec as P

ITERS = 3
EPS = 1e-06
teacher_temp = 0.07
student_temp = 0.1

ALL = ("z", "y", "x", "c")
CHIPS = ("z", "y", "x")
SWAP = [(0, 1), (1, 0)]
F32 = jnp.float32
BF16 = jnp.bfloat16
MB = 1024 * 1024
NT = (((1,), (1,)), ((), ()))
VM = pl.BlockSpec(memory_space=pltpu.VMEM)
CHUNK = 256
PASS = 64


def call(kernel, out_shape, operands, vmem, scratch=(), flops=0, nbytes=0, trans=0):
    outs = out_shape if isinstance(out_shape, (tuple, list)) else (out_shape,)
    specs = tuple(VM for _ in outs)
    return pl.pallas_call(
        kernel,
        out_shape=out_shape,
        in_specs=[VM] * len(operands),
        out_specs=specs if isinstance(out_shape, (tuple, list)) else VM,
        scratch_shapes=list(scratch),
        compiler_params=pltpu.CompilerParams(vmem_limit_bytes=vmem * MB),
        cost_estimate=pl.CostEstimate(flops=flops, bytes_accessed=nbytes, transcendentals=trans),
    )(*operands)


def fold(row):
    width = row.shape[1] // 8
    return jnp.concatenate([row[:, j * width : (j + 1) * width] for j in range(8)], axis=0)


def spread(piece, ref):
    for i in range(ref.shape[0]):
        ref[i] = piece


def flat(block):
    return jnp.concatenate([block[j : j + 1, :] for j in range(8)], axis=1)


def total_row(mine, theirs):
    return flat(mine + jnp.concatenate([theirs[4:8, :], theirs[0:4, :]], axis=0))


def columns(w_block):
    wide = w_block.astype(F32)
    inv = lax.rsqrt(jnp.sum(wide * wide, axis=0, keepdims=True) + EPS)
    return wide * inv, inv


def teacher_rows_kernel(hid_ref, proj_ref, out_ref):
    t_hid = jnp.dot(hid_ref[...], proj_ref[...], preferred_element_type=F32)
    t_bot = (t_hid * lax.rsqrt(jnp.sum(t_hid * t_hid, axis=1, keepdims=True) + EPS)).astype(BF16)
    for i in range(out_ref.shape[0]):
        out_ref[i] = t_bot


def student_rows_kernel(hid_ref, out_ref):
    wide = hid_ref[...].astype(F32)
    out_ref[...] = (wide * lax.rsqrt(jnp.sum(wide * wide, axis=1, keepdims=True) + EPS)).astype(BF16)


def teacher_kernel(total_cols, w_ref, own_ref, other_ref, e_ref, out_ref, acc):
    half = own_ref.shape[0]
    cols = w_ref.shape[1]
    acc[...] = jnp.zeros_like(acc)

    def step(j, _):
        at = pl.ds(pl.multiple_of(j * CHUNK, CHUNK), CHUNK)
        unit, _inv = columns(w_ref[:, at])
        lhs = unit.T.astype(BF16)
        sums = jnp.zeros((CHUNK, 1), F32)
        for h, rows in enumerate((own_ref, other_ref)):
            prod = lax.dot_general(lhs, rows[...], NT, preferred_element_type=F32)
            expo = jnp.exp(prod * (1.0 / teacher_temp))
            e_ref[at, h * half : (h + 1) * half] = expo
            sums = sums + jnp.sum(expo, axis=1, keepdims=True)
        scale = 1.0 / (total_cols * sums)
        scaled = e_ref[at, :] * scale
        acc[...] += jnp.sum(scaled.reshape(CHUNK // 8, 8, 2 * half), axis=0)
        return 0

    lax.fori_loop(0, cols // CHUNK, step, 0)
    spread(fold(jnp.sum(acc[...], axis=0, keepdims=True)), out_ref)


def pass_kernel(total_cols, images, e_ref, mine_ref, theirs_ref, *rest):
    *extra, out_ref, cs_ref, weight, acc = rest
    total = total_row(mine_ref[...], theirs_ref[...])
    weight[...] = jnp.broadcast_to(1.0 / (images * total), weight.shape)
    acc[...] = jnp.zeros_like(acc)
    protos = e_ref.shape[0]
    n = e_ref.shape[1]

    def step(j, _):
        at = pl.ds(pl.multiple_of(j * PASS, PASS), PASS)
        expo = e_ref[at, :]
        weighted = expo.reshape(PASS // 8, 8, n) * weight[...][None]
        sums = jnp.sum(weighted.reshape(PASS, n), axis=1, keepdims=True)
        scale = 1.0 / (total_cols * sums)
        cs_ref[at, :] = scale
        acc[...] += jnp.sum((expo * scale).reshape(PASS // 8, 8, n), axis=0)
        return 0

    lax.fori_loop(0, protos // PASS, step, 0)
    piece = fold(jnp.sum(acc[...], axis=0, keepdims=True))
    spread(jnp.concatenate([piece] + [ref[...] for ref in extra], axis=0), out_ref)


def student_kernel(w_ref, own_ref, other_ref, lg_ref, cols_ref, out_ref, acc):
    half = own_ref.shape[0]
    cols = w_ref.shape[1]
    acc[...] = jnp.zeros_like(acc)

    def step(j, _):
        at = pl.ds(pl.multiple_of(j * CHUNK, CHUNK), CHUNK)
        unit, _inv = columns(w_ref[:, at])
        cols_ref[:, at] = unit.astype(BF16)
        lhs = unit.T.astype(BF16)
        for h, rows in enumerate((own_ref, other_ref)):
            lanes = slice(h * half, (h + 1) * half)
            prod = lax.dot_general(lhs, rows[...], NT, preferred_element_type=F32)
            logits = prod * (1.0 / student_temp)
            lg_ref[at, lanes] = logits
            acc[:, lanes] += jnp.sum(jnp.exp(logits).reshape(CHUNK // 8, 8, half), axis=0)
        return 0

    lax.fori_loop(0, cols // CHUNK, step, 0)
    out_ref[...] = fold(jnp.sum(acc[...], axis=0, keepdims=True))


def grad_kernel(
    e_ref, lg_ref, cs_ref, cols_ref, mine_ref, theirs_ref, g_ref, other_ref, loss_ref, rows
):
    protos, n = e_ref.shape
    half = n // 2
    part = total_row(mine_ref[8:16, :], theirs_ref[8:16, :])
    rows[0:1, :] = 1.0 / part
    rows[1:2, :] = 1.0 / total_row(mine_ref[0:8, :], theirs_ref[0:8, :])
    rows[2:3, :] = jnp.log(part)
    loss_ref[...] = jnp.zeros_like(loss_ref)

    def step(j, _):
        at = pl.ds(pl.multiple_of(j * PASS, PASS), PASS)
        logits = lg_ref[at, :]
        target = e_ref[at, :] * cs_ref[at, :] * rows[1:2, :]
        powers = jnp.exp(logits) * rows[0:1, :]
        g_ref[at, :] = ((powers - target) * (1.0 / student_temp)).astype(BF16)
        terms = target * (rows[2:3, :] - logits)
        folded = jnp.sum(terms.reshape(PASS // 8, 8, n), axis=0)
        loss_ref[...] += jnp.sum(folded.reshape(8, n // 128, 128), axis=1)
        return 0

    lax.fori_loop(0, protos // PASS, step, 0)
    bottleneck(cols_ref, g_ref, half, other_ref)


def bottleneck(cols_ref, g_ref, start, out_ref):
    for i in range(out_ref.shape[0] // CHUNK):
        lanes = slice(start + i * CHUNK, start + (i + 1) * CHUNK)
        block = jnp.dot(cols_ref[...], g_ref[:, lanes], preferred_element_type=F32)
        out_ref[i * CHUNK : (i + 1) * CHUNK, :] = block.T


def protos_kernel(g_ref, cols_ref, w_ref, own_ref, other_ref, dp_ref, db_ref):
    half = own_ref.shape[0]
    bottleneck(cols_ref, g_ref, 0, db_ref)

    def step(j, _):
        at = pl.ds(pl.multiple_of(j * CHUNK, CHUNK), CHUNK)
        d_unit = jnp.dot(g_ref[at, :half], own_ref[...], preferred_element_type=F32)
        d_unit = d_unit + jnp.dot(g_ref[at, half:], other_ref[...], preferred_element_type=F32)
        d_unit = d_unit.T
        unit, inv = columns(w_ref[:, at])
        dp_ref[:, at] = inv * (d_unit - unit * jnp.sum(unit * d_unit, axis=0, keepdims=True))
        return 0

    lax.fori_loop(0, w_ref.shape[1] // CHUNK, step, 0)


def pack_kernel(mine_ref, theirs_ref, loss_a, loss_b, out_ref):
    total = jnp.sum(jnp.sum(loss_a[...] + loss_b[...], axis=0, keepdims=True), axis=1, keepdims=True)
    high = total.astype(BF16).astype(F32)
    mid = (total - high).astype(BF16).astype(F32)
    low = total - high - mid
    row = lax.broadcasted_iota(jnp.int32, (8, 128), 0)
    tail = jnp.where(row == 0, high, jnp.where(row == 1, mid, jnp.where(row == 2, low, 0.0)))
    tail = tail.astype(BF16)

    def step(i, _):
        at = pl.ds(pl.multiple_of(i * 24, 8), 24)
        block = mine_ref[at, :] + theirs_ref[at, :]
        for k in range(3):
            out_ref[i, 24 * k : 24 * (k + 1), :] = block[:, 128 * k : 128 * (k + 1)].astype(BF16)
        out_ref[i, 72:80, :] = tail
        return 0

    lax.fori_loop(0, out_ref.shape[0], step, 0, unroll=4)


def finish_kernel(images, got_ref, hid_ref, ds_ref, loss_ref):
    total = jnp.sum(got_ref[...].astype(F32), axis=0)
    d_bot = jnp.concatenate([total[24 * k : 24 * (k + 1), :] for k in range(3)], axis=1)
    wide = hid_ref[...].astype(F32)
    inv = lax.rsqrt(jnp.sum(wide * wide, axis=1, keepdims=True) + EPS)
    unit = wide * inv
    ds_ref[...] = inv * (d_bot - unit * jnp.sum(unit * d_bot, axis=1, keepdims=True))
    loss_ref[...] = (total[72:73, :] + total[73:74, :] + total[74:75, :]) * (1.0 / images)


def body(teacher_hidden, teacher_proj, student_hidden, teacher_protos, student_protos):
    chips = lax.axis_size(CHIPS)
    rows_dev, bot = student_hidden.shape
    half = rows_dev * chips
    images = 2 * half
    protos = teacher_protos.shape[1]
    total_cols = protos * lax.axis_size(ALL)
    sds = jax.ShapeDtypeStruct

    def swap(x):
        return lax.ppermute(x, "c", SWAP)

    def exchange(x):
        return lax.all_to_all(x, CHIPS, 0, 0)

    def row_sums(x):
        mine = jnp.sum(exchange(x), axis=0)
        return mine, swap(mine)

    s_bot = call(student_rows_kernel, sds((rows_dev, bot), BF16), (student_hidden,), 2)
    s_own = lax.all_gather(s_bot, CHIPS, axis=0, tiled=True)
    s_bot, teacher_hidden = lax.optimization_barrier((s_bot, teacher_hidden))

    t_send = call(
        teacher_rows_kernel, sds((chips, rows_dev, bot), BF16), (teacher_hidden, teacher_proj), 6
    )
    t_own = exchange(t_send).reshape(half, bot)
    t_other = swap(t_own)

    vec = sds((chips, 8, images // 8), F32)
    expo, sent = call(
        lambda *r: teacher_kernel(total_cols, *r),
        (sds((protos, images), F32), vec),
        (teacher_protos, t_own, t_other),
        12,
        [pltpu.VMEM((8, images), F32)],
    )
    for sweep in range(1, ITERS):
        mine, theirs = row_sums(sent)
        extra = ()
        if sweep == 1:
            mine, s_own = lax.optimization_barrier((mine, s_own))
            s_other = swap(s_own)
        if sweep == ITERS - 1:
            logits, s_cols, part = call(
                student_kernel,
                (sds((protos, images), F32), sds((bot, protos), BF16), sds((8, images // 8), F32)),
                (student_protos, s_own, s_other),
                12,
                [pltpu.VMEM((8, images), F32)],
            )
            extra = (part,)
        sent, col_scale = call(
            lambda *r: pass_kernel(total_cols, images, *r),
            (sds((chips, 8 + 8 * len(extra), images // 8), F32), sds((protos, 1), F32)),
            (expo, mine, theirs) + extra,
            6,
            [pltpu.VMEM((8, images), F32), pltpu.VMEM((8, images), F32)],
        )
    mine, theirs = row_sums(sent)
    grads, d_other, loss_mine = call(
        grad_kernel,
        (sds((protos, images), BF16), sds((half, bot), F32), sds((8, 128), F32)),
        (expo, logits, col_scale, s_cols, mine, theirs),
        12,
        [pltpu.VMEM((8, images), F32)],
    )
    d_theirs = swap(d_other)
    loss_theirs = swap(loss_mine)
    d_protos, d_mine = call(
        protos_kernel,
        (sds((bot, protos), F32), sds((half, bot), F32)),
        (grads, s_cols, student_protos, s_own, s_other),
        12,
    )
    packed = call(
        pack_kernel,
        sds((chips, 80, 128), BF16),
        (d_mine, d_theirs, loss_mine, loss_theirs),
        4,
    )
    got = exchange(packed)
    d_student, loss = call(
        lambda *r: finish_kernel(images, *r),
        (sds((rows_dev, bot), F32), sds((1, 128), F32)),
        (got, student_hidden),
        4,
    )
    return loss[0, 0], d_student, d_protos


def solution(mesh):
    grid = Mesh(mesh.devices.reshape(4, 4, 4, 2), ALL)
    return jax.shard_map(
        body,
        mesh=grid,
        in_specs=(P(ALL, None), P(), P(ALL, None), P(None, ALL), P(None, ALL)),
        out_specs=(P(), P(ALL, None), P(None, ALL)),
        check_vma=False,
    )
```

```python
import functools

import jax
import jax.numpy as jnp
from jax import lax
from jax.experimental import pallas as pl
from jax.experimental.pallas import tpu as pltpu
from jax.sharding import Mesh
from jax.sharding import PartitionSpec as P

ITERS = 3
EPS = 1e-06
teacher_temp = 0.07
student_temp = 0.1

ALL = ("z", "y", "x", "c")
CHIPS = ("z", "y", "x")
SWAP = [(0, 1), (1, 0)]
F32 = jnp.float32
BF16 = jnp.bfloat16
MB = 1024 * 1024
NT = (((1,), (1,)), ((), ()))
VM = pl.BlockSpec(memory_space=pltpu.VMEM)
CHUNK = 256
BLOCK = 128
ANY = pl.BlockSpec(memory_space=pltpu.HBM)


def call(kernel, out_shape, operands, vmem, scratch=(), in_any=(), out_any=(), flops=0, nbytes=0):
    many = isinstance(out_shape, (tuple, list))
    outs = out_shape if many else (out_shape,)
    specs = tuple(ANY if i in out_any else VM for i in range(len(outs)))
    return pl.pallas_call(
        kernel,
        out_shape=out_shape,
        in_specs=[ANY if i in in_any else VM for i in range(len(operands))],
        out_specs=specs if many else specs[0],
        scratch_shapes=list(scratch),
        compiler_params=pltpu.CompilerParams(vmem_limit_bytes=vmem * MB),
        cost_estimate=pl.CostEstimate(flops=flops, bytes_accessed=nbytes, transcendentals=0),
    )(*operands)


def fold(row):
    width = row.shape[1] // 8
    return jnp.concatenate([row[:, j * width : (j + 1) * width] for j in range(8)], axis=0)


def spread(piece, ref):
    piece = piece.astype(ref.dtype)
    for i in range(ref.shape[0]):
        ref[i] = piece


def flat(block):
    return jnp.concatenate([block[j : j + 1, :] for j in range(8)], axis=1)


def total_row(mine, theirs):
    return flat(mine + jnp.concatenate([theirs[4:8, :], theirs[0:4, :]], axis=0))


def columns(w_block):
    wide = w_block.astype(F32)
    inv = lax.rsqrt(jnp.sum(wide * wide, axis=0, keepdims=True) + EPS)
    return wide * inv, inv


def rows_kernel(s_ref, hid_ref, proj_ref, send_ref, s_buf, hid_buf, proj_buf, sem):
    parts = proj_buf.shape[0]
    depth = proj_buf.shape[1]
    first = pltpu.make_async_copy(s_ref, s_buf, sem.at[0])
    second = pltpu.make_async_copy(hid_ref, hid_buf, sem.at[1])
    copies = [
        pltpu.make_async_copy(proj_ref.at[pl.ds(i * depth, depth), :], proj_buf.at[i], sem.at[2 + i])
        for i in range(parts)
    ]
    first.start()
    second.start()
    for copy in copies:
        copy.start()
    first.wait()
    wide = s_buf[...].astype(F32)
    unit = wide * lax.rsqrt(jnp.sum(wide * wide, axis=1, keepdims=True) + EPS)
    second.wait()
    t_hid = jnp.zeros((hid_buf.shape[0], proj_buf.shape[2]), F32)
    for i, copy in enumerate(copies):
        copy.wait()
        t_hid = t_hid + jnp.dot(
            hid_buf[:, i * depth : (i + 1) * depth], proj_buf[i], preferred_element_type=F32
        )
    t_bot = t_hid * lax.rsqrt(jnp.sum(t_hid * t_hid, axis=1, keepdims=True) + EPS)
    spread(jnp.concatenate([t_bot, unit], axis=1), send_ref)


def sum_kernel(got_ref, out_ref):
    out_ref[...] = jnp.sum(got_ref[...].astype(F32), axis=0)


def own_kernel(tw_ref, sw_ref, rows_ref, e_ref, lg_ref, t_lhs, s_lhs, s_cols, sums_ref, part_ref):
    part_ref[...] = jnp.zeros_like(part_ref)

    def step(j, _):
        at = pl.ds(pl.multiple_of(j * CHUNK, CHUNK), CHUNK)
        t_lhs[at, :] = columns(tw_ref[:, at])[0].T.astype(BF16)
        unit = columns(sw_ref[:, at])[0]
        s_cols[:, at] = unit.astype(BF16)
        s_lhs[at, :] = unit.T.astype(BF16)
        sums_ref[at, :] = products(at, t_lhs, s_lhs, rows_ref, e_ref, lg_ref, part_ref)
        return 0

    lax.fori_loop(0, tw_ref.shape[1] // CHUNK, step, 0)


def products(at, t_lhs, s_lhs, rows_ref, e_ref, lg_ref, part_ref):
    bot = t_lhs.shape[1]
    expo = jnp.exp(
        lax.dot_general(t_lhs[at, :], rows_ref[:, :bot], NT, preferred_element_type=F32) * (1.0 / teacher_temp)
    )
    e_ref[at, :] = expo
    logits = lax.dot_general(s_lhs[at, :], rows_ref[:, bot:], NT, preferred_element_type=F32) * (1.0 / student_temp)
    lg_ref[at, :] = logits
    part_ref[...] += jnp.sum(jnp.exp(logits).reshape(CHUNK // 8, 8, logits.shape[1]), axis=0)
    return jnp.sum(expo, axis=1, keepdims=True)


def other_kernel(
    total_cols, t_lhs, s_lhs, rows_ref, e_own, sums_ref, part_own, e_ref, lg_ref, out_ref, part, acc
):
    half = rows_ref.shape[0]
    part[...] = jnp.zeros_like(part)
    acc[...] = jnp.zeros_like(acc)

    def step(j, _):
        at = pl.ds(pl.multiple_of(j * CHUNK, CHUNK), CHUNK)
        sums = sums_ref[at, :] + products(at, t_lhs, s_lhs, rows_ref, e_ref, lg_ref, part)
        scale = 1.0 / (total_cols * sums)
        row_pass(e_own.at[at, :], scale, acc.at[:, :half])
        row_pass(e_ref.at[at, :], scale, acc.at[:, half:])
        return 0

    lax.fori_loop(0, t_lhs.shape[0] // CHUNK, step, 0)
    parts = jnp.concatenate([part_own[...], part[...]], axis=1)
    row = fold(jnp.sum(acc[...], axis=0, keepdims=True))
    spread(jnp.concatenate([row, fold(jnp.sum(parts, axis=0, keepdims=True))], axis=0), out_ref)


def row_pass(block_ref, scale, acc):
    rows, n = block_ref.shape
    scale = scale.reshape(rows // 8, 8, 1)
    for start in range(0, n, 512):
        lanes = slice(start, start + 512)
        acc[:, lanes] += jnp.sum(block_ref[:, lanes].reshape(rows // 8, 8, 512) * scale, axis=0)


def pass_kernel(total_cols, images, own_ref, other_ref, mine_ref, theirs_ref, out_ref, cs_ref, weight, acc):
    total = total_row(mine_ref[0:8, :], theirs_ref[0:8, :])
    weight[...] = jnp.broadcast_to(1.0 / (images * total), weight.shape)
    acc[...] = jnp.zeros_like(acc)
    protos, half = own_ref.shape

    def step(j, _):
        at = pl.ds(pl.multiple_of(j * BLOCK, BLOCK), BLOCK)
        sums = jnp.zeros((BLOCK, 1), F32)
        for ref, start in ((own_ref, 0), (other_ref, half)):
            weighted = ref[at, :].reshape(BLOCK // 8, 8, half) * weight[:, start : start + half][None]
            sums = sums + jnp.sum(weighted.reshape(BLOCK, half), axis=1, keepdims=True)
        scale = 1.0 / (total_cols * sums)
        cs_ref[at, :] = scale
        row_pass(own_ref.at[at, :], scale, acc.at[:, :half])
        row_pass(other_ref.at[at, :], scale, acc.at[:, half:])
        return 0

    lax.fori_loop(0, protos // BLOCK, step, 0)
    spread(fold(jnp.sum(acc[...], axis=0, keepdims=True)), out_ref)


STRIP = 32
LANES = 768


def grad_kernel(
    devices, e_own, e_other, lg_own, lg_other, cs_ref, cols_ref, first_a, first_b, last_a, last_b,
    g_own, g_other, other_ref, loss_ref, rows, acc
):
    protos, half = e_own.shape
    n = 2 * half
    part = total_row(first_a[8:16, :], first_b[8:16, :])
    row = total_row(last_a[...], last_b[...])
    rows[0:8, :] = jnp.broadcast_to((1.0 / student_temp) / part, (8, n))
    rows[8:16, :] = jnp.broadcast_to((1.0 / student_temp) / row, (8, n))
    acc[...] = jnp.zeros_like(acc)
    fold_rows = (STRIP // 8, 8, LANES)

    def step(k, _):
        at = pl.ds(pl.multiple_of(k * STRIP, STRIP), STRIP)
        scale = cs_ref[at, :]
        for e_ref, lg_ref, g_ref, offset in ((e_own, lg_own, g_own, 0), (e_other, lg_other, g_other, half)):
            for start in range(0, half, LANES):
                lanes = slice(start, start + LANES)
                wide = slice(offset + start, offset + start + LANES)
                logits = lg_ref[at, lanes]
                scaled = e_ref[at, lanes] * scale
                acc[:, wide] += jnp.sum((scaled * logits).reshape(fold_rows), axis=0)
                powers = jnp.exp(logits).reshape(fold_rows) * rows[0:8, wide][None]
                target = scaled.reshape(fold_rows) * rows[8:16, wide][None]
                g_ref[at, lanes] = (powers - target).reshape(STRIP, LANES).astype(BF16)
        return 0

    lax.fori_loop(0, protos // STRIP, step, 0)
    terms = jnp.log(part) * (1.0 / devices) - jnp.sum(acc[...], axis=0, keepdims=True) / row
    pieces = fold(terms)
    loss_ref[...] = sum(pieces[:, 128 * k : 128 * (k + 1)] for k in range(n // 1024))
    bottleneck(cols_ref, g_other, other_ref)


def bottleneck(cols_ref, g_ref, out_ref):
    for i in range(out_ref.shape[0] // CHUNK):
        at = slice(i * CHUNK, (i + 1) * CHUNK)
        block = jnp.dot(cols_ref[...], g_ref[:, at], preferred_element_type=F32)
        out_ref[at, :] = block.T


def protos_kernel(g_own, g_other, cols_ref, w_ref, own_ref, other_ref, dp_ref, db_ref):
    bot = w_ref.shape[0]
    bottleneck(cols_ref, g_own, db_ref)

    def step(j, _):
        at = pl.ds(pl.multiple_of(j * CHUNK, CHUNK), CHUNK)
        d_unit = jnp.dot(g_own[at, :], own_ref[:, bot:], preferred_element_type=F32)
        d_unit = d_unit + jnp.dot(g_other[at, :], other_ref[:, bot:], preferred_element_type=F32)
        d_unit = d_unit.T
        unit, inv = columns(w_ref[:, at])
        dp_ref[:, at] = inv * (d_unit - unit * jnp.sum(unit * d_unit, axis=0, keepdims=True))
        return 0

    lax.fori_loop(0, w_ref.shape[1] // CHUNK, step, 0)


def pack_kernel(mine_ref, theirs_ref, loss_a, loss_b, out_ref):
    total = jnp.sum(jnp.sum(loss_a[...] + loss_b[...], axis=0, keepdims=True), axis=1, keepdims=True)
    high = total.astype(BF16).astype(F32)
    mid = (total - high).astype(BF16).astype(F32)
    low = total - high - mid
    row = lax.broadcasted_iota(jnp.int32, (8, 128), 0)
    tail = jnp.where(row == 0, high, jnp.where(row == 1, mid, jnp.where(row == 2, low, 0.0)))
    tail = tail.astype(BF16)

    def step(i, _):
        at = pl.ds(pl.multiple_of(i * 24, 8), 24)
        block = mine_ref[at, :] + theirs_ref[at, :]
        for k in range(3):
            out_ref[i, 24 * k : 24 * (k + 1), :] = block[:, 128 * k : 128 * (k + 1)].astype(BF16)
        out_ref[i, 72:80, :] = tail
        return 0

    lax.fori_loop(0, out_ref.shape[0], step, 0, unroll=4)


def finish_kernel(images, got_ref, hid_ref, ds_ref, loss_ref):
    total = jnp.sum(got_ref[...].astype(F32), axis=0)
    d_bot = jnp.concatenate([total[24 * k : 24 * (k + 1), :] for k in range(3)], axis=1)
    wide = hid_ref[...].astype(F32)
    inv = lax.rsqrt(jnp.sum(wide * wide, axis=1, keepdims=True) + EPS)
    unit = wide * inv
    ds_ref[...] = inv * (d_bot - unit * jnp.sum(unit * d_bot, axis=1, keepdims=True))
    loss_ref[...] = (total[72:73, :] + total[73:74, :] + total[74:75, :]) * (1.0 / images)


def body(teacher_hidden, teacher_proj, student_hidden, teacher_protos, student_protos):
    chips = lax.axis_size(CHIPS)
    rows_dev, bot = student_hidden.shape
    half = rows_dev * chips
    images = 2 * half
    protos = teacher_protos.shape[1]
    total_cols = protos * lax.axis_size(ALL)
    sds = jax.ShapeDtypeStruct

    def swap(x):
        return lax.ppermute(x, "c", SWAP)

    def exchange(x):
        return lax.all_to_all(x, CHIPS, 0, 0)

    def row_sums(x, rows):
        mine = call(sum_kernel, sds((rows, images // 8), F32), (exchange(x),), 2)
        return mine, swap(mine)

    both = call(
        rows_kernel,
        sds((chips, rows_dev, 2 * bot), BF16),
        (student_hidden, teacher_hidden, teacher_proj),
        60,
        [
            pltpu.VMEM(student_hidden.shape, BF16),
            pltpu.VMEM(teacher_hidden.shape, BF16),
            pltpu.VMEM((4, teacher_proj.shape[0] // 4, bot), BF16),
            pltpu.SemaphoreType.DMA((6,)),
        ],
        in_any=(0, 1, 2),
    )
    own = exchange(both).reshape(half, 2 * bot)
    other = swap(own)

    matrix = sds((protos, half), F32)
    lhs = sds((protos, bot), BF16)
    column = sds((protos, 1), F32)
    part8 = sds((8, half), F32)
    fold8 = pltpu.VMEM((8, images), F32)
    e_own, lg_own, t_lhs, s_lhs, s_cols, sums, part = call(
        own_kernel,
        (matrix, matrix, lhs, lhs, sds((bot, protos), BF16), column, part8),
        (teacher_protos, student_protos, own),
        8,
    )
    e_other, lg_other, sent = call(
        functools.partial(other_kernel, total_cols),
        (matrix, matrix, sds((chips, 16, images // 8), BF16)),
        (t_lhs, s_lhs, other, e_own, sums, part),
        8,
        [pltpu.VMEM((8, half), F32), fold8],
    )
    first = row_sums(sent, 16)
    sums = first
    for sweep in range(1, ITERS):
        sent, col_scale = call(
            functools.partial(pass_kernel, total_cols, images),
            (sds((chips, 8, images // 8), BF16), column),
            (e_own, e_other) + sums,
            4,
            [fold8, fold8],
        )
        sums = row_sums(sent, 8)
    g_own, g_other, d_other, loss_mine = call(
        functools.partial(grad_kernel, 2 * chips),
        (sds((protos, half), BF16), sds((protos, half), BF16), sds((half, bot), F32), sds((8, 128), F32)),
        (e_own, e_other, lg_own, lg_other, col_scale, s_cols) + first + sums,
        4,
        [pltpu.VMEM((16, images), F32), fold8],
    )
    d_theirs = swap(d_other)
    loss_theirs = swap(loss_mine)
    d_protos, d_mine = call(
        protos_kernel,
        (sds((bot, protos), F32), sds((half, bot), F32)),
        (g_own, g_other, s_cols, student_protos, own, other),
        12,
    )
    packed = call(
        pack_kernel,
        sds((chips, 80, 128), BF16),
        (d_mine, d_theirs, loss_mine, loss_theirs),
        4,
    )
    got = exchange(packed)
    d_student, loss = call(
        functools.partial(finish_kernel, images),
        (sds((rows_dev, bot), F32), sds((1, 128), F32)),
        (got, student_hidden),
        4,
    )
    return loss[0, 0], d_student, d_protos


def solution(mesh):
    grid = Mesh(mesh.devices.reshape(4, 4, 4, 2), ALL)
    return jax.shard_map(
        body,
        mesh=grid,
        in_specs=(P(ALL, None), P(), P(ALL, None), P(None, ALL), P(None, ALL)),
        out_specs=(P(), P(ALL, None), P(None, ALL)),
        check_vma=False,
    )
```

```python
import functools

import jax
import jax.numpy as jnp
from jax import lax
from jax.experimental import pallas as pl
from jax.experimental.pallas import tpu as pltpu
from jax.sharding import Mesh
from jax.sharding import PartitionSpec as P

ITERS = 3
EPS = 1e-06
teacher_temp = 0.07
student_temp = 0.1

ALL = ("z", "y", "x", "c")
CHIPS = ("z", "y", "x")
SWAP = [(0, 1), (1, 0)]
F32 = jnp.float32
BF16 = jnp.bfloat16
MB = 1024 * 1024
NT = (((1,), (1,)), ((), ()))
VM = pl.BlockSpec(memory_space=pltpu.VMEM)
CHUNK = 256
BLOCK = 256
ANY = pl.BlockSpec(memory_space=pltpu.HBM)


def call(kernel, out_shape, operands, vmem, scratch=(), in_any=(), out_any=(), flops=0, nbytes=0):
    many = isinstance(out_shape, (tuple, list))
    outs = out_shape if many else (out_shape,)
    specs = tuple(ANY if i in out_any else VM for i in range(len(outs)))
    return pl.pallas_call(
        kernel,
        out_shape=out_shape,
        in_specs=[ANY if i in in_any else VM for i in range(len(operands))],
        out_specs=specs if many else specs[0],
        scratch_shapes=list(scratch),
        compiler_params=pltpu.CompilerParams(vmem_limit_bytes=vmem * MB),
        cost_estimate=pl.CostEstimate(flops=flops, bytes_accessed=nbytes, transcendentals=0),
    )(*operands)


def fold(row):
    width = row.shape[1] // 8
    return jnp.concatenate([row[:, j * width : (j + 1) * width] for j in range(8)], axis=0)


def spread(piece, ref):
    piece = piece.astype(ref.dtype)
    for i in range(ref.shape[0]):
        ref[i] = piece


def flat(block):
    return jnp.concatenate([block[j : j + 1, :] for j in range(8)], axis=1)


def total_row(mine, theirs):
    return flat(mine + jnp.concatenate([theirs[4:8, :], theirs[0:4, :]], axis=0))


def columns(w_block):
    wide = w_block.astype(F32)
    inv = lax.rsqrt(jnp.sum(wide * wide, axis=0, keepdims=True) + EPS)
    return wide * inv, inv


def rows_kernel(s_ref, hid_ref, proj_ref, send_ref, s_buf, hid_buf, proj_buf, sem):
    parts = proj_buf.shape[0]
    depth = proj_buf.shape[1]
    first = pltpu.make_async_copy(s_ref, s_buf, sem.at[0])
    second = pltpu.make_async_copy(hid_ref, hid_buf, sem.at[1])
    copies = [
        pltpu.make_async_copy(proj_ref.at[pl.ds(i * depth, depth), :], proj_buf.at[i], sem.at[2 + i])
        for i in range(parts)
    ]
    first.start()
    second.start()
    for copy in copies:
        copy.start()
    first.wait()
    wide = s_buf[...].astype(F32)
    unit = wide * lax.rsqrt(jnp.sum(wide * wide, axis=1, keepdims=True) + EPS)
    second.wait()
    t_hid = jnp.zeros((hid_buf.shape[0], proj_buf.shape[2]), F32)
    for i, copy in enumerate(copies):
        copy.wait()
        t_hid = t_hid + jnp.dot(
            hid_buf[:, i * depth : (i + 1) * depth], proj_buf[i], preferred_element_type=F32
        )
    t_bot = t_hid * lax.rsqrt(jnp.sum(t_hid * t_hid, axis=1, keepdims=True) + EPS)
    spread(jnp.concatenate([t_bot, unit], axis=1), send_ref)


def sum_kernel(got_ref, out_ref):
    out_ref[...] = jnp.sum(got_ref[...].astype(F32), axis=0)


def chunks(total, size):
    return [slice(j, j + size) for j in range(0, total, size)]


def own_kernel(tw_ref, sw_ref, rows_ref, e_ref, lg_ref, t_lhs, s_lhs, s_cols, sums_ref, part_ref):
    part_ref[...] = jnp.zeros_like(part_ref)
    for at in chunks(tw_ref.shape[1], CHUNK):
        t_lhs[at, :] = columns(tw_ref[:, at])[0].T.astype(BF16)
        unit = columns(sw_ref[:, at])[0]
        s_cols[:, at] = unit.astype(BF16)
        s_lhs[at, :] = unit.T.astype(BF16)
        sums_ref[at, :] = products(at, t_lhs, s_lhs, rows_ref, e_ref, lg_ref, part_ref)


def products(at, t_lhs, s_lhs, rows_ref, e_ref, lg_ref, part_ref):
    bot = t_lhs.shape[1]
    expo = jnp.exp(
        lax.dot_general(t_lhs[at, :], rows_ref[:, :bot], NT, preferred_element_type=F32) * (1.0 / teacher_temp)
    )
    e_ref[at, :] = expo
    logits = lax.dot_general(s_lhs[at, :], rows_ref[:, bot:], NT, preferred_element_type=F32) * (1.0 / student_temp)
    lg_ref[at, :] = logits
    part_ref[...] += jnp.sum(jnp.exp(logits).reshape(CHUNK // 8, 8, logits.shape[1]), axis=0)
    return jnp.sum(expo, axis=1, keepdims=True)


def other_kernel(
    total_cols, t_lhs, s_lhs, rows_ref, e_own, sums_ref, part_own, e_ref, lg_ref, out_ref, part, acc
):
    half = rows_ref.shape[0]
    part[...] = jnp.zeros_like(part)
    acc[...] = jnp.zeros_like(acc)
    for at in chunks(t_lhs.shape[0], CHUNK):
        sums = sums_ref[at, :] + products(at, t_lhs, s_lhs, rows_ref, e_ref, lg_ref, part)
        scale = 1.0 / (total_cols * sums)
        row_pass(e_own.at[at, :], scale, acc.at[:, :half])
        row_pass(e_ref.at[at, :], scale, acc.at[:, half:])
    parts = jnp.concatenate([part_own[...], part[...]], axis=1)
    row = fold(jnp.sum(acc[...], axis=0, keepdims=True))
    spread(jnp.concatenate([row, fold(jnp.sum(parts, axis=0, keepdims=True))], axis=0), out_ref)


def row_pass(block_ref, scale, acc):
    rows, n = block_ref.shape
    scale = scale.reshape(rows // 8, 8, 1)
    for start in range(0, n, 512):
        lanes = slice(start, start + 512)
        acc[:, lanes] += jnp.sum(block_ref[:, lanes].reshape(rows // 8, 8, 512) * scale, axis=0)


def pass_kernel(total_cols, images, own_ref, other_ref, mine_ref, theirs_ref, out_ref, cs_ref, weight, acc):
    total = total_row(mine_ref[0:8, :], theirs_ref[0:8, :])
    weight[...] = jnp.broadcast_to(1.0 / (images * total), weight.shape)
    acc[...] = jnp.zeros_like(acc)
    protos, half = own_ref.shape

    def step(j, _):
        at = pl.ds(pl.multiple_of(j * BLOCK, BLOCK), BLOCK)
        sums = jnp.zeros((BLOCK, 1), F32)
        for ref, start in ((own_ref, 0), (other_ref, half)):
            weighted = ref[at, :].reshape(BLOCK // 8, 8, half) * weight[:, start : start + half][None]
            sums = sums + jnp.sum(weighted.reshape(BLOCK, half), axis=1, keepdims=True)
        scale = 1.0 / (total_cols * sums)
        cs_ref[at, :] = scale
        row_pass(own_ref.at[at, :], scale, acc.at[:, :half])
        row_pass(other_ref.at[at, :], scale, acc.at[:, half:])
        return 0

    lax.fori_loop(0, protos // BLOCK, step, 0)
    spread(fold(jnp.sum(acc[...], axis=0, keepdims=True)), out_ref)


STRIP = 32


def grad_kernel(
    devices, e_own, e_other, lg_own, lg_other, cs_ref, cols_ref, first_a, first_b, last_a, last_b,
    g_own, g_other, other_ref, loss_ref, rows, acc
):
    protos, half = e_own.shape
    n = 2 * half
    part = total_row(first_a[8:16, :], first_b[8:16, :])
    row = total_row(last_a[...], last_b[...])
    rows[0:8, :] = jnp.broadcast_to((1.0 / student_temp) / part, (8, n))
    rows[8:16, :] = jnp.broadcast_to((1.0 / student_temp) / row, (8, n))
    acc[...] = jnp.zeros_like(acc)

    def piece(at, lanes, wide, e_ref, lg_ref, g_ref):
        logits = lg_ref[at, lanes]
        scaled = e_ref[at, lanes] * cs_ref[at, :]
        folded = (STRIP // 8, 8, logits.shape[1])
        acc[:, wide] += jnp.sum((scaled * logits).reshape(folded), axis=0)
        powers = jnp.exp(logits).reshape(folded) * rows[0:8, wide][None]
        target = scaled.reshape(folded) * rows[8:16, wide][None]
        g_ref[at, lanes] = (powers - target).reshape(logits.shape).astype(BF16)

    def step(k, _):
        at = pl.ds(pl.multiple_of(k * STRIP, STRIP), STRIP)
        for lanes in chunks(half, half // 2):
            piece(at, lanes, slice(half + lanes.start, half + lanes.stop), e_other, lg_other, g_other)
        return 0

    lax.fori_loop(0, protos // STRIP, step, 0, unroll=2)
    for lanes in chunks(half, CHUNK):
        for at in chunks(protos, STRIP):
            piece(at, lanes, lanes, e_own, lg_own, g_own)
        bottleneck(lanes, cols_ref, g_other, other_ref)
    terms = jnp.log(part) * (1.0 / devices) - jnp.sum(acc[...], axis=0, keepdims=True) / row
    pieces = fold(terms)
    loss_ref[...] = sum(pieces[:, lanes] for lanes in chunks(n // 8, 128))


def bottleneck(lanes, cols_ref, g_ref, out_ref):
    out_ref[lanes, :] = jnp.dot(cols_ref[...], g_ref[:, lanes], preferred_element_type=F32).T


def protos_kernel(g_own, g_other, cols_ref, w_ref, own_ref, other_ref, dp_ref, db_ref, rows):
    bot = w_ref.shape[0]
    half = own_ref.shape[0]
    for lanes in chunks(half, CHUNK):
        bottleneck(lanes, cols_ref, g_own, db_ref)
    rows[:, :half] = own_ref[:, bot:].T
    rows[:, half:] = other_ref[:, bot:].T
    for at in chunks(w_ref.shape[1], CHUNK):
        d_unit = lax.dot_general(rows[:, :half], g_own[at, :], NT, preferred_element_type=F32)
        d_unit = d_unit + lax.dot_general(rows[:, half:], g_other[at, :], NT, preferred_element_type=F32)
        unit, inv = columns(w_ref[:, at])
        dp_ref[:, at] = inv * (d_unit - unit * jnp.sum(unit * d_unit, axis=0, keepdims=True))


def pack_kernel(mine_ref, theirs_ref, loss_a, loss_b, out_ref):
    total = jnp.sum(jnp.sum(loss_a[...] + loss_b[...], axis=0, keepdims=True), axis=1, keepdims=True)
    high = total.astype(BF16).astype(F32)
    mid = (total - high).astype(BF16).astype(F32)
    low = total - high - mid
    row = lax.broadcasted_iota(jnp.int32, (8, 128), 0)
    tail = jnp.where(row == 0, high, jnp.where(row == 1, mid, jnp.where(row == 2, low, 0.0)))
    tail = tail.astype(BF16)

    def step(i, _):
        at = pl.ds(pl.multiple_of(i * 24, 8), 24)
        block = mine_ref[at, :] + theirs_ref[at, :]
        for k in range(3):
            out_ref[i, 24 * k : 24 * (k + 1), :] = block[:, 128 * k : 128 * (k + 1)].astype(BF16)
        out_ref[i, 72:80, :] = tail
        return 0

    lax.fori_loop(0, out_ref.shape[0], step, 0, unroll=4)


def finish_kernel(images, got_ref, hid_ref, ds_ref, loss_ref):
    total = jnp.sum(got_ref[...].astype(F32), axis=0)
    d_bot = jnp.concatenate([total[24 * k : 24 * (k + 1), :] for k in range(3)], axis=1)
    wide = hid_ref[...].astype(F32)
    inv = lax.rsqrt(jnp.sum(wide * wide, axis=1, keepdims=True) + EPS)
    unit = wide * inv
    ds_ref[...] = inv * (d_bot - unit * jnp.sum(unit * d_bot, axis=1, keepdims=True))
    loss_ref[...] = (total[72:73, :] + total[73:74, :] + total[74:75, :]) * (1.0 / images)


def body(teacher_hidden, teacher_proj, student_hidden, teacher_protos, student_protos):
    chips = lax.axis_size(CHIPS)
    rows_dev, bot = student_hidden.shape
    half = rows_dev * chips
    images = 2 * half
    protos = teacher_protos.shape[1]
    total_cols = protos * lax.axis_size(ALL)
    sds = jax.ShapeDtypeStruct

    def swap(x):
        return lax.ppermute(x, "c", SWAP)

    def exchange(x):
        return lax.all_to_all(x, CHIPS, 0, 0)

    def row_sums(x, rows):
        mine = call(sum_kernel, sds((rows, images // 8), F32), (exchange(x),), 2)
        return mine, swap(mine)

    both = call(
        rows_kernel,
        sds((chips, rows_dev, 2 * bot), BF16),
        (student_hidden, teacher_hidden, teacher_proj),
        60,
        [
            pltpu.VMEM(student_hidden.shape, BF16),
            pltpu.VMEM(teacher_hidden.shape, BF16),
            pltpu.VMEM((4, teacher_proj.shape[0] // 4, bot), BF16),
            pltpu.SemaphoreType.DMA((6,)),
        ],
        in_any=(0, 1, 2),
    )
    own = exchange(both).reshape(half, 2 * bot)
    other = swap(own)

    matrix = sds((protos, half), F32)
    lhs = sds((protos, bot), BF16)
    column = sds((protos, 1), F32)
    part8 = sds((8, half), F32)
    fold8 = pltpu.VMEM((8, images), F32)
    e_own, lg_own, t_lhs, s_lhs, s_cols, sums, part = call(
        own_kernel,
        (matrix, matrix, lhs, lhs, sds((bot, protos), BF16), column, part8),
        (teacher_protos, student_protos, own),
        8,
    )
    e_other, lg_other, sent = call(
        functools.partial(other_kernel, total_cols),
        (matrix, matrix, sds((chips, 16, images // 8), BF16)),
        (t_lhs, s_lhs, other, e_own, sums, part),
        8,
        [pltpu.VMEM((8, half), F32), fold8],
    )
    first = row_sums(sent, 16)
    sums = first
    for sweep in range(1, ITERS):
        sent, col_scale = call(
            functools.partial(pass_kernel, total_cols, images),
            (sds((chips, 8, images // 8), BF16), column),
            (e_own, e_other) + sums,
            4,
            [fold8, fold8],
        )
        sums = row_sums(sent, 8)
    g_own, g_other, d_other, loss_mine = call(
        functools.partial(grad_kernel, 2 * chips),
        (sds((protos, half), BF16), sds((protos, half), BF16), sds((half, bot), F32), sds((8, 128), F32)),
        (e_own, e_other, lg_own, lg_other, col_scale, s_cols) + first + sums,
        4,
        [pltpu.VMEM((16, images), F32), fold8],
    )
    d_theirs = swap(d_other)
    loss_theirs = swap(loss_mine)
    d_protos, d_mine = call(
        protos_kernel,
        (sds((bot, protos), F32), sds((half, bot), F32)),
        (g_own, g_other, s_cols, student_protos, own, other),
        12,
        [pltpu.VMEM((bot, images), BF16)],
    )
    packed = call(
        pack_kernel,
        sds((chips, 80, 128), BF16),
        (d_mine, d_theirs, loss_mine, loss_theirs),
        4,
    )
    got = exchange(packed)
    d_student, loss = call(
        functools.partial(finish_kernel, images),
        (sds((rows_dev, bot), F32), sds((1, 128), F32)),
        (got, student_hidden),
        4,
    )
    return loss[0, 0], d_student, d_protos


def solution(mesh):
    grid = Mesh(mesh.devices.reshape(4, 4, 4, 2), ALL)
    return jax.shard_map(
        body,
        mesh=grid,
        in_specs=(P(ALL, None), P(), P(ALL, None), P(None, ALL), P(None, ALL)),
        out_specs=(P(), P(ALL, None), P(None, ALL)),
        check_vma=False,
    )
```

```python
import functools

import jax
import jax.numpy as jnp
from jax import lax
from jax.experimental import pallas as pl
from jax.experimental.pallas import tpu as pltpu
from jax.sharding import Mesh
from jax.sharding import PartitionSpec as P

ITERS = 3
EPS = 1e-06
teacher_temp = 0.07
student_temp = 0.1

ALL = ("z", "y", "x", "c")
CHIPS = ("z", "y", "x")
SWAP = [(0, 1), (1, 0)]
F32 = jnp.float32
BF16 = jnp.bfloat16
MB = 1024 * 1024
NT = (((1,), (1,)), ((), ()))
VM = pl.BlockSpec(memory_space=pltpu.VMEM)
CHUNK = 256
BLOCK = 256
ANY = pl.BlockSpec(memory_space=pltpu.HBM)


def call(kernel, out_shape, operands, vmem, scratch=(), in_any=(), out_any=(), flops=0, nbytes=0):
    many = isinstance(out_shape, (tuple, list))
    outs = out_shape if many else (out_shape,)
    specs = tuple(ANY if i in out_any else VM for i in range(len(outs)))
    return pl.pallas_call(
        kernel,
        out_shape=out_shape,
        in_specs=[ANY if i in in_any else VM for i in range(len(operands))],
        out_specs=specs if many else specs[0],
        scratch_shapes=list(scratch),
        compiler_params=pltpu.CompilerParams(vmem_limit_bytes=vmem * MB),
        cost_estimate=pl.CostEstimate(flops=flops, bytes_accessed=nbytes, transcendentals=0),
    )(*operands)


def fold(row):
    width = row.shape[1] // 8
    return jnp.concatenate([row[:, j * width : (j + 1) * width] for j in range(8)], axis=0)


def spread(piece, ref):
    piece = piece.astype(ref.dtype)
    for i in range(ref.shape[0]):
        ref[i] = piece


def flat(block):
    return jnp.concatenate([block[j : j + 1, :] for j in range(block.shape[0])], axis=1)


def half_rows(mine, theirs):
    return flat(jnp.concatenate([mine, theirs], axis=0))


def total_row(mine, theirs):
    return flat(mine + jnp.concatenate([theirs[4:8, :], theirs[0:4, :]], axis=0))


def columns(w_block):
    wide = w_block.astype(F32)
    inv = lax.rsqrt(jnp.sum(wide * wide, axis=0, keepdims=True) + EPS)
    return wide * inv, inv


def rows_kernel(s_ref, hid_ref, proj_ref, send_ref, s_buf, hid_buf, proj_buf, sem):
    parts = proj_buf.shape[0]
    depth = proj_buf.shape[1]
    first = pltpu.make_async_copy(s_ref, s_buf, sem.at[0])
    second = pltpu.make_async_copy(hid_ref, hid_buf, sem.at[1])
    copies = [
        pltpu.make_async_copy(proj_ref.at[pl.ds(i * depth, depth), :], proj_buf.at[i], sem.at[2 + i])
        for i in range(parts)
    ]
    first.start()
    second.start()
    for copy in copies:
        copy.start()
    first.wait()
    wide = s_buf[...].astype(F32)
    unit = wide * lax.rsqrt(jnp.sum(wide * wide, axis=1, keepdims=True) + EPS)
    second.wait()
    t_hid = jnp.zeros((hid_buf.shape[0], proj_buf.shape[2]), F32)
    for i, copy in enumerate(copies):
        copy.wait()
        t_hid = t_hid + jnp.dot(
            hid_buf[:, i * depth : (i + 1) * depth], proj_buf[i], preferred_element_type=F32
        )
    t_bot = t_hid * lax.rsqrt(jnp.sum(t_hid * t_hid, axis=1, keepdims=True) + EPS)
    spread(jnp.concatenate([t_bot, unit], axis=1), send_ref)


def sum_kernel(got_ref, out_ref):
    out_ref[...] = jnp.sum(got_ref[...].astype(F32), axis=0)


def chunks(total, size):
    return [slice(j, j + size) for j in range(0, total, size)]


def own_kernel(tw_ref, sw_ref, rows_ref, e_ref, lg_ref, t_lhs, s_lhs, s_cols, sums_ref, part_ref):
    part_ref[...] = jnp.zeros_like(part_ref)
    for at in chunks(tw_ref.shape[1], CHUNK):
        t_lhs[at, :] = columns(tw_ref[:, at])[0].T.astype(BF16)
        unit = columns(sw_ref[:, at])[0]
        s_cols[:, at] = unit.astype(BF16)
        s_lhs[at, :] = unit.T.astype(BF16)
        sums_ref[at, :] = products(at, t_lhs, s_lhs, rows_ref, e_ref, lg_ref, part_ref)


def products(at, t_lhs, s_lhs, rows_ref, e_ref, lg_ref, part_ref):
    bot = t_lhs.shape[1]
    expo = jnp.exp(
        lax.dot_general(t_lhs[at, :], rows_ref[:, :bot], NT, preferred_element_type=F32) * (1.0 / teacher_temp)
    )
    e_ref[at, :] = expo
    logits = lax.dot_general(s_lhs[at, :], rows_ref[:, bot:], NT, preferred_element_type=F32) * (1.0 / student_temp)
    lg_ref[at, :] = logits
    part_ref[...] += jnp.sum(jnp.exp(logits).reshape(CHUNK // 8, 8, logits.shape[1]), axis=0)
    return jnp.sum(expo, axis=1, keepdims=True)


def other_kernel(total_cols, t_lhs, s_lhs, rows_ref, sums_ref, e_ref, lg_ref, cs_ref, out_ref, part, acc):
    part[...] = jnp.zeros_like(part)
    acc[...] = jnp.zeros_like(acc)
    for at in chunks(t_lhs.shape[0], CHUNK):
        sums = sums_ref[at, :] + products(at, t_lhs, s_lhs, rows_ref, e_ref, lg_ref, part)
        scale = 1.0 / (total_cols * sums)
        cs_ref[at, :] = scale
        row_pass(e_ref.at[at, :], scale, acc)
    out_ref[...] = fold_pair(acc[...], part[...])


def fold_pair(rows, parts):
    both = jnp.concatenate([jnp.sum(rows, axis=0, keepdims=True), jnp.sum(parts, axis=0, keepdims=True)], axis=1)
    return fold(both)


def own_rows_kernel(e_ref, cs_ref, part_ref, out_ref, acc):
    acc[...] = jnp.zeros_like(acc)
    row_pass(e_ref, cs_ref[...], acc)
    out_ref[...] = fold_pair(acc[...], part_ref[...])


def send_kernel(mine_ref, theirs_ref, out_ref):
    spread(mine_ref[...] + theirs_ref[...], out_ref)


def turn_kernel(rows_ref, out_ref):
    out_ref[...] = rows_ref[:, out_ref.shape[0] :].T


def row_pass(block_ref, scale, acc):
    rows, n = block_ref.shape
    scale = scale.reshape(rows // 8, 8, 1)
    for start in range(0, n, 512):
        lanes = slice(start, start + 512)
        acc[:, lanes] += jnp.sum(block_ref[:, lanes].reshape(rows // 8, 8, 512) * scale, axis=0)


def pass_kernel(total_cols, images, first, own_ref, other_ref, mine_ref, theirs_ref, out_ref, cs_ref, weight, acc):
    if first:
        total = half_rows(mine_ref[0:4, :], theirs_ref[0:4, :])
    else:
        total = total_row(mine_ref[...], theirs_ref[...])
    weight[...] = jnp.broadcast_to(1.0 / (images * total), weight.shape)
    acc[...] = jnp.zeros_like(acc)
    protos, half = own_ref.shape

    def step(j, _):
        at = pl.ds(pl.multiple_of(j * BLOCK, BLOCK), BLOCK)
        sums = jnp.zeros((BLOCK, 1), F32)
        for ref, start in ((own_ref, 0), (other_ref, half)):
            weighted = ref[at, :].reshape(BLOCK // 8, 8, half) * weight[:, start : start + half][None]
            sums = sums + jnp.sum(weighted.reshape(BLOCK, half), axis=1, keepdims=True)
        scale = 1.0 / (total_cols * sums)
        cs_ref[at, :] = scale
        row_pass(own_ref.at[at, :], scale, acc.at[:, :half])
        row_pass(other_ref.at[at, :], scale, acc.at[:, half:])
        return 0

    lax.fori_loop(0, protos // BLOCK, step, 0)
    spread(fold(jnp.sum(acc[...], axis=0, keepdims=True)), out_ref)


STRIP = 32
DEPTH = 512


def half_gradients(row, part, e_ref, lg_ref, cs_ref, cols_ref, turned_ref, db_ref, unit_sum, start, g, rows, cross):
    protos, half = e_ref.shape
    rows[0:8, :] = jnp.broadcast_to((1.0 / student_temp) / part, (8, half))
    rows[8:16, :] = jnp.broadcast_to((1.0 / student_temp) / row, (8, half))
    folded = (STRIP // 8, 8, CHUNK)
    for _, _, acc in cross:
        acc[...] = jnp.zeros_like(acc)

    def elementwise(lanes):
        for at in chunks(protos, STRIP):
            for expo, logits, acc in cross:
                scaled = expo[at, lanes] * cs_ref[at, :]
                acc[:, lanes] += jnp.sum((scaled * logits[at, lanes]).reshape(folded), axis=0)
            logits = lg_ref[at, lanes]
            scaled = e_ref[at, lanes] * cs_ref[at, :]
            powers = jnp.exp(logits).reshape(folded) * rows[0:8, lanes][None]
            target = scaled.reshape(folded) * rows[8:16, lanes][None]
            g[at, lanes] = (powers - target).reshape(logits.shape).astype(BF16)

    def matmuls(lanes):
        db_ref[lanes, :] = jnp.dot(cols_ref[...], g[:, lanes], preferred_element_type=F32).T
        if lanes.stop % DEPTH == 0:
            deep = slice(lanes.stop - DEPTH, lanes.stop)
            term = lax.dot_general(turned_ref[:, deep], g[:, deep], NT, preferred_element_type=F32)
            if lanes.stop > DEPTH:
                unit_sum[...] += term
            else:
                unit_sum[...] = term if start is None else start[...] + term

    before = None
    for lanes in chunks(half, CHUNK):
        elementwise(lanes)
        if before is not None:
            matmuls(before)
        before = lanes
    matmuls(before)


def grad_other_kernel(
    devices, e_ref, lg_ref, cs_ref, cols_ref, turned_ref, part_own, part_other, mine_ref, theirs_ref, e_own, lg_own,
    db_ref, unit_sum, loss_ref, g, rows, acc, acc_own
):
    row = flat(mine_ref[4:8, :] + theirs_ref[0:4, :])
    part = flat(part_other[4:8, :])
    cross = ((e_ref, lg_ref, acc), (e_own, lg_own, acc_own))
    half_gradients(row, part, e_ref, lg_ref, cs_ref, cols_ref, turned_ref, db_ref, unit_sum, None, g, rows, cross)
    parts = jnp.log(part) + jnp.log(flat(part_own[4:8, :]))
    row_own = flat(mine_ref[0:4, :] + theirs_ref[4:8, :])
    crossed = jnp.sum(acc[...], axis=0, keepdims=True) / row + jnp.sum(acc_own[...], axis=0, keepdims=True) / row_own
    terms = parts * (1.0 / devices) - crossed
    loss_ref[...] = sum(terms[:, lanes] for lanes in chunks(terms.shape[1], 128))


def grad_own_kernel(
    e_ref, lg_ref, cs_ref, cols_ref, turned_ref, part_ref, mine_ref, theirs_ref, other_sum, w_ref,
    db_ref, dp_ref, g, rows, unit_sum, out_buf, sem
):
    row = flat(mine_ref[0:4, :] + theirs_ref[4:8, :])
    part = flat(part_ref[4:8, :])
    half_gradients(row, part, e_ref, lg_ref, cs_ref, cols_ref, turned_ref, db_ref, unit_sum, other_sum, g, rows, ())
    copies = []
    for j, at in enumerate(chunks(w_ref.shape[1], CHUNK)):
        d_unit = unit_sum[:, at]
        unit, inv = columns(w_ref[:, at])
        out_buf[:, at] = inv * (d_unit - unit * jnp.sum(unit * d_unit, axis=0, keepdims=True))
        copies.append(pltpu.make_async_copy(out_buf.at[:, at], dp_ref.at[:, at], sem.at[j]))
        copies[j].start()
    for copy in copies:
        copy.wait()


def pack_kernel(mine_ref, theirs_ref, loss_a, loss_b, out_ref):
    total = jnp.sum(loss_a[...] + loss_b[...], axis=1, keepdims=True)
    high = total.astype(BF16).astype(F32)
    mid = (total - high).astype(BF16).astype(F32)
    low = total - high - mid
    row = lax.broadcasted_iota(jnp.int32, (8, 128), 0)
    tail = jnp.where(row == 0, high, jnp.where(row == 1, mid, jnp.where(row == 2, low, 0.0)))
    tail = tail.astype(BF16)

    def step(i, _):
        at = pl.ds(pl.multiple_of(i * 24, 8), 24)
        block = mine_ref[at, :] + theirs_ref[at, :]
        for k in range(3):
            out_ref[i, 24 * k : 24 * (k + 1), :] = block[:, 128 * k : 128 * (k + 1)].astype(BF16)
        out_ref[i, 72:80, :] = tail
        return 0

    lax.fori_loop(0, out_ref.shape[0], step, 0, unroll=4)


def finish_kernel(images, got_ref, hid_ref, ds_ref, loss_ref):
    total = jnp.sum(got_ref[...].astype(F32), axis=0)
    d_bot = jnp.concatenate([total[24 * k : 24 * (k + 1), :] for k in range(3)], axis=1)
    wide = hid_ref[...].astype(F32)
    inv = lax.rsqrt(jnp.sum(wide * wide, axis=1, keepdims=True) + EPS)
    unit = wide * inv
    ds_ref[...] = inv * (d_bot - unit * jnp.sum(unit * d_bot, axis=1, keepdims=True))
    loss_ref[...] = (total[72:73, :] + total[73:74, :] + total[74:75, :]) * (1.0 / images)


def body(teacher_hidden, teacher_proj, student_hidden, teacher_protos, student_protos):
    chips = lax.axis_size(CHIPS)
    rows_dev, bot = student_hidden.shape
    half = rows_dev * chips
    images = 2 * half
    protos = teacher_protos.shape[1]
    total_cols = protos * lax.axis_size(ALL)
    sds = jax.ShapeDtypeStruct

    def swap(x):
        return lax.ppermute(x, "c", SWAP)

    def exchange(x):
        return lax.all_to_all(x, CHIPS, 0, 0)

    def row_sums(x, rows):
        mine = call(sum_kernel, sds((rows, images // 8), F32), (exchange(x),), 2)
        return mine, swap(mine)

    both = call(
        rows_kernel,
        sds((chips, rows_dev, 2 * bot), BF16),
        (student_hidden, teacher_hidden, teacher_proj),
        60,
        [
            pltpu.VMEM(student_hidden.shape, BF16),
            pltpu.VMEM(teacher_hidden.shape, BF16),
            pltpu.VMEM((4, teacher_proj.shape[0] // 4, bot), BF16),
            pltpu.SemaphoreType.DMA((6,)),
        ],
        in_any=(0, 1, 2),
    )
    own = exchange(both).reshape(half, 2 * bot)
    other = swap(own)

    matrix = sds((protos, half), F32)
    lhs = sds((protos, bot), BF16)
    column = sds((protos, 1), F32)
    part8 = sds((8, half), F32)
    fold8 = pltpu.VMEM((8, images), F32)
    e_own, lg_own, t_lhs, s_lhs, s_cols, sums, part = call(
        own_kernel,
        (matrix, matrix, lhs, lhs, sds((bot, protos), BF16), column, part8),
        (teacher_protos, student_protos, own),
        8,
    )
    half8 = sds((8, images // 8), F32)
    send8 = sds((chips, 8, images // 8), BF16)
    half_acc = pltpu.VMEM((8, half), F32)
    part, own_late = lax.optimization_barrier((part, own))
    turned_own = call(turn_kernel, sds((bot, half), BF16), (own_late,), 2)
    other, turned_own = lax.optimization_barrier((other, turned_own))
    e_other, lg_other, col_scale, pair_other = call(
        functools.partial(other_kernel, total_cols),
        (matrix, matrix, column, half8),
        (t_lhs, s_lhs, other, sums),
        8,
        [half_acc, half_acc],
    )
    theirs = swap(pair_other)
    pair_own = call(own_rows_kernel, half8, (e_own, col_scale, part), 4, [half_acc])
    first = row_sums(call(send_kernel, send8, (pair_own, theirs), 2), 8)
    kept, late = lax.optimization_barrier((first[0], other))
    turned_other = call(turn_kernel, sds((bot, half), BF16), (late,), 2)
    theirs, turned_other = lax.optimization_barrier((first[1], turned_other))
    first = (kept, theirs)
    sums = first
    for sweep in range(1, ITERS):
        sent, col_scale = call(
            functools.partial(pass_kernel, total_cols, images, sweep == 1),
            (send8, column),
            (e_own, e_other) + sums,
            4,
            [fold8, fold8],
        )
        sums = row_sums(sent, 8)
    tile = sds((1, 128), F32)
    grads = [pltpu.VMEM((protos, half), BF16), pltpu.VMEM((16, half), F32)]
    d_other, unit_sum, loss_mine = call(
        functools.partial(grad_other_kernel, 2 * chips),
        (sds((half, bot), F32), sds((bot, protos), F32), tile),
        (e_other, lg_other, col_scale, s_cols, turned_other) + first + sums + (e_own, lg_own),
        8,
        grads + [half_acc, half_acc],
    )
    d_theirs = swap(d_other)
    loss_theirs = swap(loss_mine)
    whole = pltpu.VMEM((bot, protos), F32)
    d_mine, d_protos = call(
        grad_own_kernel,
        (sds((half, bot), F32), sds((bot, protos), F32)),
        (e_own, lg_own, col_scale, s_cols, turned_own, first[0]) + sums + (unit_sum, student_protos),
        12,
        grads + [whole, whole, pltpu.SemaphoreType.DMA((protos // CHUNK,))],
        out_any=(1,),
    )
    packed = call(
        pack_kernel,
        sds((chips, 80, 128), BF16),
        (d_mine, d_theirs, loss_mine, loss_theirs),
        4,
    )
    got = exchange(packed)
    d_student, loss = call(
        functools.partial(finish_kernel, images),
        (sds((rows_dev, bot), F32), sds((1, 128), F32)),
        (got, student_hidden),
        4,
    )
    return loss[0, 0], d_student, d_protos


def solution(mesh):
    grid = Mesh(mesh.devices.reshape(4, 4, 4, 2), ALL)
    return jax.shard_map(
        body,
        mesh=grid,
        in_specs=(P(ALL, None), P(), P(ALL, None), P(None, ALL), P(None, ALL)),
        out_specs=(P(), P(ALL, None), P(None, ALL)),
        check_vma=False,
    )
```

```python
import functools

import jax
import jax.numpy as jnp
from jax import lax
from jax.experimental import pallas as pl
from jax.experimental.pallas import tpu as pltpu
from jax.sharding import Mesh
from jax.sharding import PartitionSpec as P

ITERS = 3
EPS = 1e-06
teacher_temp = 0.07
student_temp = 0.1

ALL = ("z", "y", "x", "c")
CHIPS = ("z", "y", "x")
SWAP = [(0, 1), (1, 0)]
F32 = jnp.float32
BF16 = jnp.bfloat16
MB = 1024 * 1024
NT = (((1,), (1,)), ((), ()))
VM = pl.BlockSpec(memory_space=pltpu.VMEM)
CHUNK = 256
BLOCK = 256
ANY = pl.BlockSpec(memory_space=pltpu.HBM)


def call(kernel, out_shape, operands, vmem, scratch=(), in_any=(), out_any=(), flops=0, nbytes=0):
    many = isinstance(out_shape, (tuple, list))
    outs = out_shape if many else (out_shape,)
    specs = tuple(ANY if i in out_any else VM for i in range(len(outs)))
    return pl.pallas_call(
        kernel,
        out_shape=out_shape,
        in_specs=[ANY if i in in_any else VM for i in range(len(operands))],
        out_specs=specs if many else specs[0],
        scratch_shapes=list(scratch),
        compiler_params=pltpu.CompilerParams(vmem_limit_bytes=vmem * MB),
        cost_estimate=pl.CostEstimate(flops=flops, bytes_accessed=nbytes, transcendentals=0),
    )(*operands)


def fold(row):
    width = row.shape[1] // 8
    return jnp.concatenate([row[:, j * width : (j + 1) * width] for j in range(8)], axis=0)


def spread(piece, ref):
    piece = piece.astype(ref.dtype)
    for i in range(ref.shape[0]):
        ref[i] = piece


def flat(block):
    return jnp.concatenate([block[j : j + 1, :] for j in range(block.shape[0])], axis=1)


def total_row(mine, theirs):
    return flat(mine + jnp.concatenate([theirs[4:8, :], theirs[0:4, :]], axis=0))


def columns(w_block):
    wide = w_block.astype(F32)
    inv = lax.rsqrt(jnp.sum(wide * wide, axis=0, keepdims=True) + EPS)
    return wide * inv, inv


def rows_kernel(s_ref, hid_ref, proj_ref, send_ref, s_out_ref, s_buf, hid_buf, proj_buf, sem):
    parts = proj_buf.shape[0]
    depth = proj_buf.shape[1]
    first = pltpu.make_async_copy(s_ref, s_buf, sem.at[0])
    second = pltpu.make_async_copy(hid_ref, hid_buf, sem.at[1])
    copies = [
        pltpu.make_async_copy(proj_ref.at[pl.ds(i * depth, depth), :], proj_buf.at[i], sem.at[2 + i])
        for i in range(parts)
    ]
    first.start()
    second.start()
    for copy in copies:
        copy.start()
    first.wait()
    wide = s_buf[...].astype(F32)
    unit = wide * lax.rsqrt(jnp.sum(wide * wide, axis=1, keepdims=True) + EPS)
    s_out_ref[...] = unit.astype(BF16)
    second.wait()
    t_hid = jnp.zeros((hid_buf.shape[0], proj_buf.shape[2]), F32)
    for i, copy in enumerate(copies):
        copy.wait()
        t_hid = t_hid + jnp.dot(
            hid_buf[:, i * depth : (i + 1) * depth], proj_buf[i], preferred_element_type=F32
        )
    t_bot = t_hid * lax.rsqrt(jnp.sum(t_hid * t_hid, axis=1, keepdims=True) + EPS)
    spread(t_bot, send_ref)


def sum_kernel(got_ref, out_ref):
    out_ref[...] = jnp.sum(got_ref[...].astype(F32), axis=0)


def chunks(total, size):
    return [slice(j, j + size) for j in range(0, total, size)]


def expo_block(at, lhs_ref, rows_ref, e_ref):
    prod = lax.dot_general(lhs_ref[at, :], rows_ref[...], NT, preferred_element_type=F32)
    expo = jnp.exp(prod * (1.0 / teacher_temp))
    e_ref[at, :] = expo
    return jnp.sum(expo, axis=1, keepdims=True)


def teacher_own_kernel(w_ref, rows_ref, e_ref, lhs_ref, sums_ref):
    for at in chunks(w_ref.shape[1], CHUNK):
        lhs_ref[at, :] = columns(w_ref[:, at])[0].T.astype(BF16)
        sums_ref[at, :] = expo_block(at, lhs_ref, rows_ref, e_ref)


def teacher_other_kernel(total_cols, lhs_ref, rows_ref, e_own, sums_ref, s_ref, e_ref, out_ref, acc):
    half = rows_ref.shape[0]
    acc[...] = jnp.zeros_like(acc)
    for at in chunks(lhs_ref.shape[0], CHUNK):
        scale = 1.0 / (total_cols * (sums_ref[at, :] + expo_block(at, lhs_ref, rows_ref, e_ref)))
        row_pass(e_own.at[at, :], scale, acc.at[:, :half])
        row_pass(e_ref.at[at, :], scale, acc.at[:, half:])
    sums = fold(jnp.sum(acc[...], axis=0, keepdims=True))
    spread(jnp.concatenate([sums, s_ref[...].astype(F32)], axis=0), out_ref)


def open_kernel(got_ref, sums_ref, rows_ref):
    total = jnp.zeros(sums_ref.shape, F32)
    for i in range(got_ref.shape[0]):
        piece = got_ref[i].astype(F32)
        total = total + piece[0:8, :]
        rows_ref[i] = piece[8:, :].astype(BF16)
    sums_ref[...] = total


def fold_half(part):
    row = jnp.sum(part, axis=0, keepdims=True)
    width = row.shape[1] // 4
    return jnp.concatenate([row[:, j * width : (j + 1) * width] for j in range(4)], axis=0)


def student_columns_kernel(w_ref, lhs_ref, cols_ref):
    for at in chunks(w_ref.shape[1], CHUNK):
        unit = columns(w_ref[:, at])[0]
        cols_ref[:, at] = unit.astype(BF16)
        lhs_ref[at, :] = unit.T.astype(BF16)


def student_kernel(start, lhs_ref, rows_ref, lg_ref, out_ref, part):
    part[...] = jnp.zeros_like(part)
    for at in chunks(lg_ref.shape[0], CHUNK):
        lhs = lhs_ref[start + at.start : start + at.stop, :]
        prod = lax.dot_general(lhs, rows_ref[...], NT, preferred_element_type=F32)
        logits = prod * (1.0 / student_temp)
        lg_ref[at, :] = logits
        part[...] += jnp.sum(jnp.exp(logits).reshape(CHUNK // 8, 8, logits.shape[1]), axis=0)
    out_ref[...] = fold_half(part[...])


def pair_kernel(row_ref, part_a, part_b, out_ref):
    out_ref[...] = jnp.concatenate([row_ref[4:8, :], part_a[...] + part_b[...]], axis=0)


def send_kernel(row_ref, part_a, part_b, theirs_ref, out_ref):
    spread(jnp.concatenate([row_ref[0:4, :], part_a[...] + part_b[...]], axis=0) + theirs_ref[...], out_ref)


def pick(refs, at):
    first = refs[0].shape[0]
    if at.stop <= first:
        return refs[0], at
    return refs[1], slice(at.start - first, at.stop - first)


def turn_kernel(rows_ref, out_ref):
    out_ref[...] = rows_ref[...].T


def row_pass(block_ref, scale, acc):
    rows, n = block_ref.shape
    scale = scale.reshape(rows // 8, 8, 1)
    for start in range(0, n, 512):
        lanes = slice(start, start + 512)
        acc[:, lanes] += jnp.sum(block_ref[:, lanes].reshape(rows // 8, 8, 512) * scale, axis=0)


def pass_kernel(total_cols, images, own_ref, other_ref, mine_ref, theirs_ref, out_ref, cs_ref, weight, acc):
    total = total_row(mine_ref[...], theirs_ref[...])
    weight[...] = jnp.broadcast_to(1.0 / (images * total), weight.shape)
    acc[...] = jnp.zeros_like(acc)
    protos, half = own_ref.shape

    def step(j, _):
        at = pl.ds(pl.multiple_of(j * BLOCK, BLOCK), BLOCK)
        sums = jnp.zeros((BLOCK, 1), F32)
        for ref, start in ((own_ref, 0), (other_ref, half)):
            weighted = ref[at, :].reshape(BLOCK // 8, 8, half) * weight[:, start : start + half][None]
            sums = sums + jnp.sum(weighted.reshape(BLOCK, half), axis=1, keepdims=True)
        scale = 1.0 / (total_cols * sums)
        cs_ref[at, :] = scale
        row_pass(own_ref.at[at, :], scale, acc.at[:, :half])
        row_pass(other_ref.at[at, :], scale, acc.at[:, half:])
        return 0

    lax.fori_loop(0, protos // BLOCK, step, 0)
    piece = fold(jnp.sum(acc[...], axis=0, keepdims=True))
    if len(out_ref.shape) == 3:
        spread(piece, out_ref)
    else:
        out_ref[...] = piece


STRIP = 32
DEPTH = 512


def half_gradients(row, part, e_ref, lg_ref, cs_ref, cols_ref, turned_ref, db_ref, unit_sum, start, g, rows, cross):
    protos, half = e_ref.shape
    rows[0:8, :] = jnp.broadcast_to((1.0 / student_temp) / part, (8, half))
    rows[8:16, :] = jnp.broadcast_to((1.0 / student_temp) / row, (8, half))
    folded = (STRIP // 8, 8, CHUNK)
    for _, _, acc in cross:
        acc[...] = jnp.zeros_like(acc)

    def elementwise(lanes):
        for at in chunks(protos, STRIP):
            for expo, logits, acc in cross:
                scaled = expo[at, lanes] * cs_ref[at, :]
                ref, place = pick(logits, at)
                acc[:, lanes] += jnp.sum((scaled * ref[place, lanes]).reshape(folded), axis=0)
            ref, place = pick(lg_ref, at)
            logits = ref[place, lanes]
            scaled = e_ref[at, lanes] * cs_ref[at, :]
            powers = jnp.exp(logits).reshape(folded) * rows[0:8, lanes][None]
            target = scaled.reshape(folded) * rows[8:16, lanes][None]
            g[at, lanes] = (powers - target).reshape(logits.shape).astype(BF16)

    def matmuls(lanes):
        db_ref[lanes, :] = jnp.dot(cols_ref[...], g[:, lanes], preferred_element_type=F32).T
        if lanes.stop % DEPTH == 0:
            deep = slice(lanes.stop - DEPTH, lanes.stop)
            term = lax.dot_general(turned_ref[:, deep], g[:, deep], NT, preferred_element_type=F32)
            if lanes.stop > DEPTH:
                unit_sum[...] += term
            else:
                unit_sum[...] = term if start is None else start[...] + term

    before = None
    for lanes in chunks(half, CHUNK):
        elementwise(lanes)
        if before is not None:
            matmuls(before)
        before = lanes
    matmuls(before)


def grad_other_kernel(
    devices, e_ref, lg_a, lg_b, cs_ref, cols_ref, turned_ref, mine_ref, theirs_ref, e_own, lg_own_a, lg_own_b,
    db_ref, unit_sum, loss_ref, g, rows, acc, acc_own
):
    row = flat(theirs_ref[0:4, :])
    part = flat(theirs_ref[4:8, :])
    lg_ref = (lg_a, lg_b)
    cross = ((e_ref, lg_ref, acc), (e_own, (lg_own_a, lg_own_b), acc_own))
    half_gradients(row, part, e_ref, lg_ref, cs_ref, cols_ref, turned_ref, db_ref, unit_sum, None, g, rows, cross)
    parts = jnp.log(part) + jnp.log(flat(mine_ref[4:8, :]))
    row_own = flat(mine_ref[0:4, :])
    crossed = jnp.sum(acc[...], axis=0, keepdims=True) / row + jnp.sum(acc_own[...], axis=0, keepdims=True) / row_own
    terms = parts * (1.0 / devices) - crossed
    loss_ref[...] = sum(terms[:, lanes] for lanes in chunks(terms.shape[1], 128))


def grad_own_kernel(
    e_ref, lg_a, lg_b, cs_ref, cols_ref, turned_ref, mine_ref, other_sum, w_ref,
    db_ref, dp_ref, g, rows, unit_sum, out_buf, sem
):
    row = flat(mine_ref[0:4, :])
    part = flat(mine_ref[4:8, :])
    lg_ref = (lg_a, lg_b)
    half_gradients(row, part, e_ref, lg_ref, cs_ref, cols_ref, turned_ref, db_ref, unit_sum, other_sum, g, rows, ())
    copies = []
    for j, at in enumerate(chunks(w_ref.shape[1], CHUNK)):
        d_unit = unit_sum[:, at]
        unit, inv = columns(w_ref[:, at])
        out_buf[:, at] = inv * (d_unit - unit * jnp.sum(unit * d_unit, axis=0, keepdims=True))
        copies.append(pltpu.make_async_copy(out_buf.at[:, at], dp_ref.at[:, at], sem.at[j]))
        copies[j].start()
    for copy in copies:
        copy.wait()


def pack_kernel(mine_ref, theirs_ref, loss_a, loss_b, out_ref):
    total = jnp.sum(loss_a[...] + loss_b[...], axis=1, keepdims=True)
    high = total.astype(BF16).astype(F32)
    mid = (total - high).astype(BF16).astype(F32)
    low = total - high - mid
    row = lax.broadcasted_iota(jnp.int32, (8, 128), 0)
    tail = jnp.where(row == 0, high, jnp.where(row == 1, mid, jnp.where(row == 2, low, 0.0)))
    tail = tail.astype(BF16)

    def step(i, _):
        at = pl.ds(pl.multiple_of(i * 24, 8), 24)
        block = mine_ref[at, :] + theirs_ref[at, :]
        for k in range(3):
            out_ref[i, 24 * k : 24 * (k + 1), :] = block[:, 128 * k : 128 * (k + 1)].astype(BF16)
        out_ref[i, 72:80, :] = tail
        return 0

    lax.fori_loop(0, out_ref.shape[0], step, 0, unroll=4)


def finish_kernel(images, got_ref, hid_ref, ds_ref, loss_ref):
    total = jnp.sum(got_ref[...].astype(F32), axis=0)
    d_bot = jnp.concatenate([total[24 * k : 24 * (k + 1), :] for k in range(3)], axis=1)
    wide = hid_ref[...].astype(F32)
    inv = lax.rsqrt(jnp.sum(wide * wide, axis=1, keepdims=True) + EPS)
    unit = wide * inv
    ds_ref[...] = inv * (d_bot - unit * jnp.sum(unit * d_bot, axis=1, keepdims=True))
    loss_ref[...] = (total[72:73, :] + total[73:74, :] + total[74:75, :]) * (1.0 / images)


def body(teacher_hidden, teacher_proj, student_hidden, teacher_protos, student_protos):
    chips = lax.axis_size(CHIPS)
    rows_dev, bot = student_hidden.shape
    half = rows_dev * chips
    images = 2 * half
    protos = teacher_protos.shape[1]
    total_cols = protos * lax.axis_size(ALL)
    sds = jax.ShapeDtypeStruct

    def swap(x):
        return lax.ppermute(x, "c", SWAP)

    def exchange(x):
        return lax.all_to_all(x, CHIPS, 0, 0)

    def row_sums(x, rows):
        mine = call(sum_kernel, sds((rows, images // 8), F32), (exchange(x),), 2)
        return mine, swap(mine)

    t_send, s_bot = call(
        rows_kernel,
        (sds((chips, rows_dev, bot), BF16), sds((rows_dev, bot), BF16)),
        (student_hidden, teacher_hidden, teacher_proj),
        60,
        [
            pltpu.VMEM(student_hidden.shape, BF16),
            pltpu.VMEM(teacher_hidden.shape, BF16),
            pltpu.VMEM((2, teacher_proj.shape[0] // 2, bot), BF16),
            pltpu.SemaphoreType.DMA((4,)),
        ],
        in_any=(0, 1, 2),
    )
    t_own = exchange(t_send).reshape(half, bot)
    t_other = swap(t_own)

    matrix = sds((protos, half), F32)
    lhs = sds((protos, bot), BF16)
    column = sds((protos, 1), F32)
    turned = sds((bot, half), BF16)
    vec8 = sds((8, images // 8), F32)
    vec4 = sds((4, images // 8), F32)
    send8 = sds((chips, 8, images // 8), BF16)
    fold8 = pltpu.VMEM((8, images), F32)
    half_acc = pltpu.VMEM((8, half), F32)
    scales = pltpu.VMEM((protos, 1), F32)

    e_own, t_lhs, sums = call(teacher_own_kernel, (matrix, lhs, column), (teacher_protos, t_own), 8)
    sums, student_late = lax.optimization_barrier((sums, student_protos))
    s_lhs, s_cols = call(student_columns_kernel, (lhs, sds((bot, protos), BF16)), (student_late,), 8)
    t_other, s_lhs, s_cols = lax.optimization_barrier((t_other, s_lhs, s_cols))
    e_other, sent = call(
        functools.partial(teacher_other_kernel, total_cols),
        (matrix, sds((chips, 8 + rows_dev, bot), BF16)),
        (t_lhs, t_other, e_own, sums, s_bot),
        8,
        [fold8],
    )
    mine, s_own = call(open_kernel, (vec8, sds((chips, rows_dev, bot), BF16)), (exchange(sent),), 4)
    theirs = swap(mine)
    s_own = s_own.reshape(half, bot)

    def student(start, stop, rows):
        shapes = (sds((stop - start, half), F32), vec4)
        return call(functools.partial(student_kernel, start), shapes, (s_lhs, rows), 8, [half_acc])

    split = protos * 3 // 4
    lg_own_a, part_own = student(0, split, s_own)
    theirs, part_own, s_late = lax.optimization_barrier((theirs, part_own, s_own))
    s_other = swap(s_late)
    (sent,) = call(
        functools.partial(pass_kernel, total_cols, images),
        (send8,),
        (e_own, e_other, mine, theirs),
        4,
        [scales, fold8, fold8],
    )
    mine, theirs = row_sums(sent, 8)
    late, s_late = lax.optimization_barrier((mine, s_other))
    lg_a, part_other = student(0, split, s_late)
    theirs, part_other = lax.optimization_barrier((theirs, part_other))
    row, col_scale = call(
        functools.partial(pass_kernel, total_cols, images),
        (vec8, column),
        (e_own, e_other, late, theirs),
        4,
        [fold8, fold8],
    )
    row, s_late = lax.optimization_barrier((row, s_late))
    lg_b, part_rest = student(split, protos, s_late)
    pair_other = call(pair_kernel, vec8, (row, part_other, part_rest), 2)
    pair_theirs = swap(pair_other)
    pair_other, own_late = lax.optimization_barrier((pair_other, s_own))
    lg_own_b, part_own_rest = student(split, protos, own_late)
    pair_theirs, part_own_rest = lax.optimization_barrier((pair_theirs, part_own_rest))
    mine, theirs = row_sums(call(send_kernel, send8, (row, part_own, part_own_rest, pair_theirs), 2), 8)
    mine, own_late, other_late = lax.optimization_barrier((mine, s_own, s_other))
    turned_own = call(turn_kernel, turned, (own_late,), 2)
    turned_other = call(turn_kernel, turned, (other_late,), 2)
    theirs, turned_own, turned_other = lax.optimization_barrier((theirs, turned_own, turned_other))
    tile = sds((1, 128), F32)
    grads = [pltpu.VMEM((protos, half), BF16), pltpu.VMEM((16, half), F32)]
    d_other, unit_sum, loss_mine = call(
        functools.partial(grad_other_kernel, 2 * chips),
        (sds((half, bot), F32), sds((bot, protos), F32), tile),
        (e_other, lg_a, lg_b, col_scale, s_cols, turned_other, mine, theirs, e_own, lg_own_a, lg_own_b),
        8,
        grads + [half_acc, half_acc],
    )
    d_theirs = swap(d_other)
    loss_theirs = swap(loss_mine)
    whole = pltpu.VMEM((bot, protos), F32)
    d_mine, d_protos = call(
        grad_own_kernel,
        (sds((half, bot), F32), sds((bot, protos), F32)),
        (e_own, lg_own_a, lg_own_b, col_scale, s_cols, turned_own, mine, unit_sum, student_protos),
        12,
        grads + [whole, whole, pltpu.SemaphoreType.DMA((protos // CHUNK,))],
        out_any=(1,),
    )
    packed = call(
        pack_kernel,
        sds((chips, 80, 128), BF16),
        (d_mine, d_theirs, loss_mine, loss_theirs),
        4,
    )
    got = exchange(packed)
    d_student, loss = call(
        functools.partial(finish_kernel, images),
        (sds((rows_dev, bot), F32), sds((1, 128), F32)),
        (got, student_hidden),
        4,
    )
    return loss[0, 0], d_student, d_protos


def solution(mesh):
    grid = Mesh(mesh.devices.reshape(4, 4, 4, 2), ALL)
    return jax.shard_map(
        body,
        mesh=grid,
        in_specs=(P(ALL, None), P(), P(ALL, None), P(None, ALL), P(None, ALL)),
        out_specs=(P(), P(ALL, None), P(None, ALL)),
        check_vma=False,
    )
```

```python
import functools

import jax
import jax.numpy as jnp
from jax import lax
from jax.experimental import pallas as pl
from jax.experimental.pallas import tpu as pltpu
from jax.sharding import Mesh
from jax.sharding import PartitionSpec as P

ITERS = 3
EPS = 1e-06
teacher_temp = 0.07
student_temp = 0.1

ALL = ("z", "y", "x", "c")
CHIPS = ("z", "y", "x")
SWAP = [(0, 1), (1, 0)]
F32 = jnp.float32
BF16 = jnp.bfloat16
MB = 1024 * 1024
NT = (((1,), (1,)), ((), ()))
VM = pl.BlockSpec(memory_space=pltpu.VMEM)
CHUNK = 256
BLOCK = 256
ANY = pl.BlockSpec(memory_space=pltpu.HBM)


def call(kernel, out_shape, operands, vmem, scratch=(), in_any=(), out_any=(), flops=0, nbytes=0):
    many = isinstance(out_shape, (tuple, list))
    outs = out_shape if many else (out_shape,)
    specs = tuple(ANY if i in out_any else VM for i in range(len(outs)))
    return pl.pallas_call(
        kernel,
        out_shape=out_shape,
        in_specs=[ANY if i in in_any else VM for i in range(len(operands))],
        out_specs=specs if many else specs[0],
        scratch_shapes=list(scratch),
        compiler_params=pltpu.CompilerParams(vmem_limit_bytes=vmem * MB),
        cost_estimate=pl.CostEstimate(flops=flops, bytes_accessed=nbytes, transcendentals=0),
    )(*operands)


def fold(row):
    width = row.shape[1] // 8
    return jnp.concatenate([row[:, j * width : (j + 1) * width] for j in range(8)], axis=0)


def spread(piece, ref):
    piece = piece.astype(ref.dtype)
    for i in range(ref.shape[0]):
        ref[i] = piece


def flat(block):
    return jnp.concatenate([block[j : j + 1, :] for j in range(block.shape[0])], axis=1)


def total_row(mine, theirs):
    return flat(mine + jnp.concatenate([theirs[4:8, :], theirs[0:4, :]], axis=0))


def columns(w_block):
    wide = w_block.astype(F32)
    inv = lax.rsqrt(jnp.sum(wide * wide, axis=0, keepdims=True) + EPS)
    return wide * inv, inv


def rows_kernel(s_ref, hid_ref, proj_ref, send_ref, s_out_ref, s_buf, hid_buf, proj_buf, sem):
    parts = proj_buf.shape[0]
    depth = proj_buf.shape[1]
    first = pltpu.make_async_copy(s_ref, s_buf, sem.at[0])
    second = pltpu.make_async_copy(hid_ref, hid_buf, sem.at[1])
    copies = [
        pltpu.make_async_copy(proj_ref.at[pl.ds(i * depth, depth), :], proj_buf.at[i], sem.at[2 + i])
        for i in range(parts)
    ]
    first.start()
    second.start()
    for copy in copies:
        copy.start()
    first.wait()
    wide = s_buf[...].astype(F32)
    unit = wide * lax.rsqrt(jnp.sum(wide * wide, axis=1, keepdims=True) + EPS)
    s_out_ref[...] = unit.astype(BF16)
    second.wait()
    t_hid = jnp.zeros((hid_buf.shape[0], proj_buf.shape[2]), F32)
    for i, copy in enumerate(copies):
        copy.wait()
        t_hid = t_hid + jnp.dot(
            hid_buf[:, i * depth : (i + 1) * depth], proj_buf[i], preferred_element_type=F32
        )
    t_bot = t_hid * lax.rsqrt(jnp.sum(t_hid * t_hid, axis=1, keepdims=True) + EPS)
    spread(t_bot, send_ref)


def sum_kernel(got_ref, out_ref):
    out_ref[...] = jnp.sum(got_ref[...].astype(F32), axis=0)


def chunks(total, size):
    return [slice(j, j + size) for j in range(0, total, size)]


def expo_block(at, lhs_ref, rows_ref, e_ref):
    prod = lax.dot_general(lhs_ref[at, :], rows_ref[...], NT, preferred_element_type=F32)
    expo = jnp.exp(prod * (1.0 / teacher_temp))
    e_ref[at, :] = expo
    return jnp.sum(expo, axis=1, keepdims=True)


def teacher_own_kernel(w_ref, rows_ref, e_ref, lhs_ref, sums_ref):
    for at in chunks(w_ref.shape[1], CHUNK):
        lhs_ref[at, :] = columns(w_ref[:, at])[0].T.astype(BF16)
        sums_ref[at, :] = expo_block(at, lhs_ref, rows_ref, e_ref)


def teacher_other_kernel(total_cols, lhs_ref, rows_ref, e_own, sums_ref, s_ref, e_ref, out_ref, acc):
    half = rows_ref.shape[0]
    acc[...] = jnp.zeros_like(acc)
    for at in chunks(lhs_ref.shape[0], CHUNK):
        scale = 1.0 / (total_cols * (sums_ref[at, :] + expo_block(at, lhs_ref, rows_ref, e_ref)))
        row_pass(e_own.at[at, :], scale, acc.at[:, :half])
        row_pass(e_ref.at[at, :], scale, acc.at[:, half:])
    sums = fold(jnp.sum(acc[...], axis=0, keepdims=True))
    spread(jnp.concatenate([sums, s_ref[...].astype(F32)], axis=0), out_ref)


def open_kernel(got_ref, sums_ref, rows_ref):
    total = jnp.zeros(sums_ref.shape, F32)
    for i in range(got_ref.shape[0]):
        piece = got_ref[i].astype(F32)
        total = total + piece[0:8, :]
        rows_ref[i] = piece[8:, :].astype(BF16)
    sums_ref[...] = total


def fold_half(part):
    row = jnp.sum(part, axis=0, keepdims=True)
    width = row.shape[1] // 4
    return jnp.concatenate([row[:, j * width : (j + 1) * width] for j in range(4)], axis=0)


def student_columns_kernel(w_ref, lhs_ref, cols_ref):
    for at in chunks(w_ref.shape[1], CHUNK):
        unit = columns(w_ref[:, at])[0]
        cols_ref[:, at] = unit.astype(BF16)
        lhs_ref[at, :] = unit.T.astype(BF16)


def student_kernel(start, lhs_ref, rows_ref, lg_ref, out_ref, part):
    part[...] = jnp.zeros_like(part)
    for at in chunks(lg_ref.shape[0], CHUNK):
        lhs = lhs_ref[start + at.start : start + at.stop, :]
        prod = lax.dot_general(lhs, rows_ref[...], NT, preferred_element_type=F32)
        logits = prod * (1.0 / student_temp)
        lg_ref[at, :] = logits
        part[...] += jnp.sum(jnp.exp(logits).reshape(CHUNK // 8, 8, logits.shape[1]), axis=0)
    out_ref[...] = fold_half(part[...])


def pair_kernel(row_ref, part_ref, out_ref):
    out_ref[...] = jnp.concatenate([row_ref[4:8, :], part_ref[...]], axis=0)


def send_kernel(row_ref, part_a, part_b, theirs_ref, out_ref):
    spread(jnp.concatenate([row_ref[0:4, :], part_a[...] + part_b[...]], axis=0) + theirs_ref[...], out_ref)


def pick(refs, at):
    if len(refs) == 1:
        return refs[0], at
    first = refs[0].shape[0]
    if at.stop <= first:
        return refs[0], at
    return refs[1], slice(at.start - first, at.stop - first)


def turn_kernel(rows_ref, out_ref):
    out_ref[...] = rows_ref[...].T


def row_pass(block_ref, scale, acc):
    rows, n = block_ref.shape
    scale = scale.reshape(rows // 8, 8, 1)
    for start in range(0, n, 512):
        lanes = slice(start, start + 512)
        acc[:, lanes] += jnp.sum(block_ref[:, lanes].reshape(rows // 8, 8, 512) * scale, axis=0)


def pass_kernel(total_cols, images, own_ref, other_ref, mine_ref, theirs_ref, out_ref, cs_ref, weight, acc):
    total = total_row(mine_ref[...], theirs_ref[...])
    weight[...] = jnp.broadcast_to(1.0 / (images * total), weight.shape)
    acc[...] = jnp.zeros_like(acc)
    protos, half = own_ref.shape

    def step(j, _):
        at = pl.ds(pl.multiple_of(j * BLOCK, BLOCK), BLOCK)
        sums = jnp.zeros((BLOCK, 1), F32)
        for ref, start in ((own_ref, 0), (other_ref, half)):
            weighted = ref[at, :].reshape(BLOCK // 8, 8, half) * weight[:, start : start + half][None]
            sums = sums + jnp.sum(weighted.reshape(BLOCK, half), axis=1, keepdims=True)
        scale = 1.0 / (total_cols * sums)
        cs_ref[at, :] = scale
        row_pass(own_ref.at[at, :], scale, acc.at[:, :half])
        row_pass(other_ref.at[at, :], scale, acc.at[:, half:])
        return 0

    lax.fori_loop(0, protos // BLOCK, step, 0)
    piece = fold(jnp.sum(acc[...], axis=0, keepdims=True))
    if len(out_ref.shape) == 3:
        spread(piece, out_ref)
    else:
        out_ref[...] = piece


STRIP = 32
DEPTH = 512


def half_gradients(
    row, part, e_ref, lg_ref, cs_ref, cols_ref, turned_ref, db_ref, unit_sum, start, g, rows, cross, last=None
):
    protos, half = e_ref.shape
    rows[0:8, :] = jnp.broadcast_to((1.0 / student_temp) / part, (8, half))
    rows[8:16, :] = jnp.broadcast_to((1.0 / student_temp) / row, (8, half))
    folded = (STRIP // 8, 8, CHUNK)
    for _, _, acc in cross:
        acc[...] = jnp.zeros_like(acc)

    def elementwise(lanes):
        for at in chunks(protos, STRIP):
            for expo, logits, acc in cross:
                scaled = expo[at, lanes] * cs_ref[at, :]
                ref, place = pick(logits, at)
                acc[:, lanes] += jnp.sum((scaled * ref[place, lanes]).reshape(folded), axis=0)
            ref, place = pick(lg_ref, at)
            logits = ref[place, lanes]
            scaled = e_ref[at, lanes] * cs_ref[at, :]
            powers = jnp.exp(logits).reshape(folded) * rows[0:8, lanes][None]
            target = scaled.reshape(folded) * rows[8:16, lanes][None]
            g[at, lanes] = (powers - target).reshape(logits.shape).astype(BF16)

    def matmuls(lanes):
        db_ref[lanes, :] = jnp.dot(cols_ref[...], g[:, lanes], preferred_element_type=F32).T
        if lanes.stop % DEPTH == 0:
            deep = slice(lanes.stop - DEPTH, lanes.stop)
            if last is not None and lanes.stop == half:
                for at in chunks(protos, CHUNK):
                    term = lax.dot_general(turned_ref[:, deep], g[at, deep], NT, preferred_element_type=F32)
                    last(at, unit_sum[:, at] + term)
                return
            term = lax.dot_general(turned_ref[:, deep], g[:, deep], NT, preferred_element_type=F32)
            if lanes.stop > DEPTH:
                unit_sum[...] += term
            else:
                unit_sum[...] = term if start is None else start[...] + term

    before = None
    for lanes in chunks(half, CHUNK):
        elementwise(lanes)
        if before is not None:
            matmuls(before)
        before = lanes
    matmuls(before)


def grad_other_kernel(
    devices, e_ref, lg_other, cs_ref, cols_ref, turned_ref, mine_ref, theirs_ref, e_own, lg_own_a, lg_own_b,
    db_ref, unit_sum, loss_ref, g, rows, acc, acc_own
):
    row = flat(theirs_ref[0:4, :])
    part = flat(theirs_ref[4:8, :])
    lg_ref = (lg_other,)
    cross = ((e_ref, lg_ref, acc), (e_own, (lg_own_a, lg_own_b), acc_own))
    half_gradients(row, part, e_ref, lg_ref, cs_ref, cols_ref, turned_ref, db_ref, unit_sum, None, g, rows, cross)
    parts = jnp.log(part) + jnp.log(flat(mine_ref[4:8, :]))
    row_own = flat(mine_ref[0:4, :])
    crossed = jnp.sum(acc[...], axis=0, keepdims=True) / row + jnp.sum(acc_own[...], axis=0, keepdims=True) / row_own
    terms = parts * (1.0 / devices) - crossed
    loss_ref[...] = sum(terms[:, lanes] for lanes in chunks(terms.shape[1], loss_ref.shape[1]))
    db_ref[e_ref.shape[1] :, :] = jnp.broadcast_to(loss_ref[...], (8, loss_ref.shape[1]))


def grad_own_kernel(
    e_ref, lg_a, lg_b, cs_ref, cols_ref, turned_ref, mine_ref, other_sum, w_ref,
    db_ref, dp_ref, g, rows, unit_sum, out_buf, sem
):
    row = flat(mine_ref[0:4, :])
    part = flat(mine_ref[4:8, :])
    lg_ref = (lg_a, lg_b)
    copies = []

    def project(at, d_unit):
        unit, inv = columns(w_ref[:, at])
        out_buf[:, at] = inv * (d_unit - unit * jnp.sum(unit * d_unit, axis=0, keepdims=True))
        j = len(copies)
        copies.append(pltpu.make_async_copy(out_buf.at[:, at], dp_ref.at[:, at], sem.at[j]))
        copies[j].start()

    half_gradients(
        row, part, e_ref, lg_ref, cs_ref, cols_ref, turned_ref, db_ref, unit_sum, other_sum, g, rows, (), project
    )
    for copy in copies:
        copy.wait()


def pack_kernel(mine_ref, theirs_ref, loss_ref, out_ref):
    rows = mine_ref.shape[0]
    total = jnp.sum(loss_ref[...] + theirs_ref[rows : rows + 1, :], axis=1, keepdims=True)
    high = total.astype(BF16).astype(F32)
    mid = (total - high).astype(BF16).astype(F32)
    low = total - high - mid
    row = lax.broadcasted_iota(jnp.int32, (8, 128), 0)
    tail = jnp.where(row == 0, high, jnp.where(row == 1, mid, jnp.where(row == 2, low, 0.0)))
    tail = tail.astype(BF16)

    def step(i, _):
        at = pl.ds(pl.multiple_of(i * 24, 8), 24)
        block = mine_ref[at, :] + theirs_ref[at, :]
        for k in range(3):
            out_ref[i, 24 * k : 24 * (k + 1), :] = block[:, 128 * k : 128 * (k + 1)].astype(BF16)
        out_ref[i, 72:80, :] = tail
        return 0

    lax.fori_loop(0, out_ref.shape[0], step, 0, unroll=4)


def finish_kernel(images, got_ref, hid_ref, ds_ref, loss_ref):
    total = jnp.sum(got_ref[...].astype(F32), axis=0)
    d_bot = jnp.concatenate([total[24 * k : 24 * (k + 1), :] for k in range(3)], axis=1)
    wide = hid_ref[...].astype(F32)
    inv = lax.rsqrt(jnp.sum(wide * wide, axis=1, keepdims=True) + EPS)
    unit = wide * inv
    ds_ref[...] = inv * (d_bot - unit * jnp.sum(unit * d_bot, axis=1, keepdims=True))
    loss_ref[...] = (total[72:73, :] + total[73:74, :] + total[74:75, :]) * (1.0 / images)


def body(teacher_hidden, teacher_proj, student_hidden, teacher_protos, student_protos):
    chips = lax.axis_size(CHIPS)
    rows_dev, bot = student_hidden.shape
    half = rows_dev * chips
    images = 2 * half
    protos = teacher_protos.shape[1]
    total_cols = protos * lax.axis_size(ALL)
    sds = jax.ShapeDtypeStruct

    def swap(x):
        return lax.ppermute(x, "c", SWAP)

    def exchange(x):
        return lax.all_to_all(x, CHIPS, 0, 0)

    def row_sums(x, rows):
        mine = call(sum_kernel, sds((rows, images // 8), F32), (exchange(x),), 2)
        return mine, swap(mine)

    t_send, s_bot = call(
        rows_kernel,
        (sds((chips, rows_dev, bot), BF16), sds((rows_dev, bot), BF16)),
        (student_hidden, teacher_hidden, teacher_proj),
        60,
        [
            pltpu.VMEM(student_hidden.shape, BF16),
            pltpu.VMEM(teacher_hidden.shape, BF16),
            pltpu.VMEM((2, teacher_proj.shape[0] // 2, bot), BF16),
            pltpu.SemaphoreType.DMA((4,)),
        ],
        in_any=(0, 1, 2),
    )
    t_own = exchange(t_send).reshape(half, bot)
    t_other = swap(t_own)

    matrix = sds((protos, half), F32)
    lhs = sds((protos, bot), BF16)
    column = sds((protos, 1), F32)
    turned = sds((bot, half), BF16)
    vec8 = sds((8, images // 8), F32)
    vec4 = sds((4, images // 8), F32)
    send8 = sds((chips, 8, images // 8), BF16)
    fold8 = pltpu.VMEM((8, images), F32)
    half_acc = pltpu.VMEM((8, half), F32)
    scales = pltpu.VMEM((protos, 1), F32)

    e_own, t_lhs, sums = call(teacher_own_kernel, (matrix, lhs, column), (teacher_protos, t_own), 8)
    sums, student_late = lax.optimization_barrier((sums, student_protos))
    s_lhs, s_cols = call(student_columns_kernel, (lhs, sds((bot, protos), BF16)), (student_late,), 8)
    t_other, s_lhs, s_cols = lax.optimization_barrier((t_other, s_lhs, s_cols))
    e_other, sent = call(
        functools.partial(teacher_other_kernel, total_cols),
        (matrix, sds((chips, 8 + rows_dev, bot), BF16)),
        (t_lhs, t_other, e_own, sums, s_bot),
        8,
        [fold8],
    )
    mine, s_own = call(open_kernel, (vec8, sds((chips, rows_dev, bot), BF16)), (exchange(sent),), 4)
    theirs = swap(mine)
    s_own = s_own.reshape(half, bot)

    def student(start, stop, rows):
        shapes = (sds((stop - start, half), F32), vec4)
        return call(functools.partial(student_kernel, start), shapes, (s_lhs, rows), 8, [half_acc])

    split = protos * 3 // 4
    lg_own_a, part_own = student(0, split, s_own)
    theirs, part_own, s_late = lax.optimization_barrier((theirs, part_own, s_own))
    s_other = swap(s_late)
    (sent,) = call(
        functools.partial(pass_kernel, total_cols, images),
        (send8,),
        (e_own, e_other, mine, theirs),
        4,
        [scales, fold8, fold8],
    )
    mine, theirs = row_sums(sent, 8)
    late, s_late = lax.optimization_barrier((mine, s_other))
    lg_other, part_other = student(0, protos, s_late)
    theirs, part_other = lax.optimization_barrier((theirs, part_other))
    row, col_scale = call(
        functools.partial(pass_kernel, total_cols, images),
        (vec8, column),
        (e_own, e_other, late, theirs),
        4,
        [fold8, fold8],
    )
    pair_other = call(pair_kernel, vec8, (row, part_other), 2)
    pair_theirs = swap(pair_other)
    pair_other, own_late = lax.optimization_barrier((pair_other, s_own))
    lg_own_b, part_own_rest = student(split, protos, own_late)
    pair_theirs, part_own_rest = lax.optimization_barrier((pair_theirs, part_own_rest))
    mine, theirs = row_sums(call(send_kernel, send8, (row, part_own, part_own_rest, pair_theirs), 2), 8)
    mine, own_late, other_late = lax.optimization_barrier((mine, s_own, s_other))
    turned_own = call(turn_kernel, turned, (own_late,), 2)
    turned_other = call(turn_kernel, turned, (other_late,), 2)
    theirs, turned_own, turned_other = lax.optimization_barrier((theirs, turned_own, turned_other))
    tile = sds((1, bot), F32)
    grads = [pltpu.VMEM((protos, half), BF16), pltpu.VMEM((16, half), F32)]
    d_other, unit_sum, loss_mine = call(
        functools.partial(grad_other_kernel, 2 * chips),
        (sds((half + 8, bot), F32), sds((bot, protos), F32), tile),
        (e_other, lg_other, col_scale, s_cols, turned_other, mine, theirs, e_own, lg_own_a, lg_own_b),
        8,
        grads + [half_acc, half_acc],
    )
    d_theirs = swap(d_other)
    whole = pltpu.VMEM((bot, protos), F32)
    d_mine, d_protos = call(
        grad_own_kernel,
        (sds((half, bot), F32), sds((bot, protos), F32)),
        (e_own, lg_own_a, lg_own_b, col_scale, s_cols, turned_own, mine, unit_sum, student_protos),
        12,
        grads + [whole, whole, pltpu.SemaphoreType.DMA((protos // CHUNK,))],
        out_any=(1,),
    )
    packed = call(
        pack_kernel,
        sds((chips, 80, 128), BF16),
        (d_mine, d_theirs, loss_mine),
        4,
    )
    got = exchange(packed)
    d_student, loss = call(
        functools.partial(finish_kernel, images),
        (sds((rows_dev, bot), F32), sds((1, 128), F32)),
        (got, student_hidden),
        4,
    )
    return loss[0, 0], d_student, d_protos


def solution(mesh):
    grid = Mesh(mesh.devices.reshape(4, 4, 4, 2), ALL)
    return jax.shard_map(
        body,
        mesh=grid,
        in_specs=(P(ALL, None), P(), P(ALL, None), P(None, ALL), P(None, ALL)),
        out_specs=(P(), P(ALL, None), P(None, ALL)),
        check_vma=False,
    )
```

```python
import functools

import jax
import jax.numpy as jnp
from jax import lax
from jax.experimental import pallas as pl
from jax.experimental.pallas import tpu as pltpu
from jax.sharding import Mesh
from jax.sharding import PartitionSpec as P

ITERS = 3
EPS = 1e-06
teacher_temp = 0.07
student_temp = 0.1

ALL = ("z", "y", "x", "c")
CHIPS = ("z", "y", "x")
SWAP = [(0, 1), (1, 0)]
F32 = jnp.float32
BF16 = jnp.bfloat16
MB = 1024 * 1024
NT = (((1,), (1,)), ((), ()))
VM = pl.BlockSpec(memory_space=pltpu.VMEM)
CHUNK = 256
BLOCK = 256
ANY = pl.BlockSpec(memory_space=pltpu.HBM)


def call(kernel, out_shape, operands, vmem, scratch=(), in_any=(), out_any=(), flops=0, nbytes=0):
    many = isinstance(out_shape, (tuple, list))
    outs = out_shape if many else (out_shape,)
    specs = tuple(ANY if i in out_any else VM for i in range(len(outs)))
    return pl.pallas_call(
        kernel,
        out_shape=out_shape,
        in_specs=[ANY if i in in_any else VM for i in range(len(operands))],
        out_specs=specs if many else specs[0],
        scratch_shapes=list(scratch),
        compiler_params=pltpu.CompilerParams(vmem_limit_bytes=vmem * MB),
        cost_estimate=pl.CostEstimate(flops=flops, bytes_accessed=nbytes, transcendentals=0),
    )(*operands)


def fold(row):
    width = row.shape[1] // 8
    return jnp.concatenate([row[:, j * width : (j + 1) * width] for j in range(8)], axis=0)


def spread(piece, ref):
    piece = piece.astype(ref.dtype)
    for i in range(ref.shape[0]):
        ref[i] = piece


def flat(block):
    return jnp.concatenate([block[j : j + 1, :] for j in range(block.shape[0])], axis=1)


def total_row(mine, theirs):
    return flat(mine + jnp.concatenate([theirs[4:8, :], theirs[0:4, :]], axis=0))


def columns(w_block):
    wide = w_block.astype(F32)
    inv = lax.rsqrt(jnp.sum(wide * wide, axis=0, keepdims=True) + EPS)
    return wide * inv, inv


def rows_kernel(s_ref, hid_ref, proj_ref, send_ref, s_out_ref, s_buf, hid_buf, proj_buf, sem):
    parts = proj_buf.shape[0]
    depth = proj_buf.shape[1]
    first = pltpu.make_async_copy(s_ref, s_buf, sem.at[0])
    second = pltpu.make_async_copy(hid_ref, hid_buf, sem.at[1])
    copies = [
        pltpu.make_async_copy(proj_ref.at[pl.ds(i * depth, depth), :], proj_buf.at[i], sem.at[2 + i])
        for i in range(parts)
    ]
    first.start()
    second.start()
    for copy in copies:
        copy.start()
    first.wait()
    wide = s_buf[...].astype(F32)
    unit = wide * lax.rsqrt(jnp.sum(wide * wide, axis=1, keepdims=True) + EPS)
    s_out_ref[...] = unit.astype(BF16)
    second.wait()
    t_hid = jnp.zeros((hid_buf.shape[0], proj_buf.shape[2]), F32)
    for i, copy in enumerate(copies):
        copy.wait()
        t_hid = t_hid + jnp.dot(
            hid_buf[:, i * depth : (i + 1) * depth], proj_buf[i], preferred_element_type=F32
        )
    t_bot = t_hid * lax.rsqrt(jnp.sum(t_hid * t_hid, axis=1, keepdims=True) + EPS)
    spread(t_bot, send_ref)


def sum_kernel(got_ref, out_ref):
    out_ref[...] = jnp.sum(got_ref[...].astype(F32), axis=0)


def chunks(total, size):
    return [slice(j, j + size) for j in range(0, total, size)]


def expo_block(at, lhs_ref, rows_ref, e_ref):
    prod = lax.dot_general(lhs_ref[at, :], rows_ref[...], NT, preferred_element_type=F32)
    expo = jnp.exp(prod * (1.0 / teacher_temp))
    e_ref[at, :] = expo
    return jnp.sum(expo, axis=1, keepdims=True)


def teacher_own_kernel(w_ref, rows_ref, e_ref, lhs_ref, sums_ref):
    for at in chunks(w_ref.shape[1], CHUNK):
        lhs_ref[at, :] = columns(w_ref[:, at])[0].T.astype(BF16)
        sums_ref[at, :] = expo_block(at, lhs_ref, rows_ref, e_ref)


def teacher_other_kernel(total_cols, expected, lhs_ref, rows_ref, e_own, sums_ref, s_ref, e_ref, out_ref, acc):
    half = rows_ref.shape[0]
    acc[...] = jnp.zeros_like(acc)
    for at in chunks(lhs_ref.shape[0], CHUNK):
        scale = 1.0 / (total_cols * (sums_ref[at, :] + expo_block(at, lhs_ref, rows_ref, e_ref)))
        row_pass(e_own.at[at, :], scale, acc.at[:, :half])
        row_pass(e_ref.at[at, :], scale, acc.at[:, half:])
    sums = fold(jnp.sum(acc[...], axis=0, keepdims=True)) - expected
    spread(jnp.concatenate([sums, s_ref[...].astype(F32)], axis=0), out_ref)


def open_kernel(got_ref, sums_ref, rows_ref):
    total = jnp.zeros(sums_ref.shape, F32)
    for i in range(got_ref.shape[0]):
        piece = got_ref[i].astype(F32)
        total = total + piece[0:8, :]
        rows_ref[i] = piece[8:, :].astype(BF16)
    sums_ref[...] = total


def fold_half(part):
    row = jnp.sum(part, axis=0, keepdims=True)
    width = row.shape[1] // 4
    return jnp.concatenate([row[:, j * width : (j + 1) * width] for j in range(4)], axis=0)


def student_columns_kernel(w_ref, lhs_ref, cols_ref):
    for at in chunks(w_ref.shape[1], CHUNK):
        unit = columns(w_ref[:, at])[0]
        cols_ref[:, at] = unit.astype(BF16)
        lhs_ref[at, :] = unit.T.astype(BF16)


def student_kernel(start, lhs_ref, rows_ref, lg_ref, out_ref, part):
    part[...] = jnp.zeros_like(part)
    for at in chunks(lg_ref.shape[0], CHUNK):
        lhs = lhs_ref[start + at.start : start + at.stop, :]
        prod = lax.dot_general(lhs, rows_ref[...], NT, preferred_element_type=F32)
        logits = prod * (1.0 / student_temp)
        lg_ref[at, :] = logits
        part[...] += jnp.sum(jnp.exp(logits).reshape(CHUNK // 8, 8, logits.shape[1]), axis=0)
    out_ref[...] = fold_half(part[...])


def pair_kernel(row_ref, part_ref, out_ref):
    out_ref[...] = jnp.concatenate([row_ref[4:8, :], part_ref[...]], axis=0)


def send_kernel(row_ref, part_a, part_b, theirs_ref, out_ref):
    spread(jnp.concatenate([row_ref[0:4, :], part_a[...] + part_b[...]], axis=0) + theirs_ref[...], out_ref)


def pick(refs, at):
    if len(refs) == 1:
        return refs[0], at
    first = refs[0].shape[0]
    if at.stop <= first:
        return refs[0], at
    return refs[1], slice(at.start - first, at.stop - first)


def turn_kernel(rows_ref, out_ref):
    out_ref[...] = rows_ref[...].T


def row_pass(block_ref, scale, acc):
    rows, n = block_ref.shape
    scale = scale.reshape(rows // 8, 8, 1)
    for start in range(0, n, 512):
        lanes = slice(start, start + 512)
        acc[:, lanes] += jnp.sum(block_ref[:, lanes].reshape(rows // 8, 8, 512) * scale, axis=0)


def pass_kernel(total_cols, images, devices, own_ref, other_ref, mine_ref, theirs_ref, *rest):
    *before, out_ref, total_ref, cs_ref, weight, acc = rest
    total = total_row(mine_ref[...], theirs_ref[...])
    total = total + (flat(before[0][...]) if before else 1.0 / images)
    total_ref[...] = fold(total)
    weight[...] = jnp.broadcast_to(1.0 / (images * total), weight.shape)
    acc[...] = jnp.zeros_like(acc)
    protos, half = own_ref.shape

    def step(j, _):
        at = pl.ds(pl.multiple_of(j * BLOCK, BLOCK), BLOCK)
        sums = jnp.zeros((BLOCK, 1), F32)
        for ref, start in ((own_ref, 0), (other_ref, half)):
            weighted = ref[at, :].reshape(BLOCK // 8, 8, half) * weight[:, start : start + half][None]
            sums = sums + jnp.sum(weighted.reshape(BLOCK, half), axis=1, keepdims=True)
        scale = 1.0 / (total_cols * sums)
        cs_ref[at, :] = scale
        row_pass(own_ref.at[at, :], scale, acc.at[:, :half])
        row_pass(other_ref.at[at, :], scale, acc.at[:, half:])
        return 0

    lax.fori_loop(0, protos // BLOCK, step, 0)
    piece = fold(jnp.sum(acc[...], axis=0, keepdims=True)) - total_ref[...] * (1.0 / devices)
    if len(out_ref.shape) == 3:
        spread(piece, out_ref)
    else:
        out_ref[...] = piece


STRIP = 32
DEPTH = 512


def half_gradients(
    row, part, e_ref, lg_ref, cs_ref, cols_ref, turned_ref, db_ref, unit_sum, start, g, rows, cross, last=None
):
    protos, half = e_ref.shape
    rows[0:8, :] = jnp.broadcast_to((1.0 / student_temp) / part, (8, half))
    rows[8:16, :] = jnp.broadcast_to((1.0 / student_temp) / row, (8, half))
    folded = (STRIP // 8, 8, CHUNK)
    for _, _, acc in cross:
        acc[...] = jnp.zeros_like(acc)

    def elementwise(lanes):
        for at in chunks(protos, STRIP):
            for expo, logits, acc in cross:
                scaled = expo[at, lanes] * cs_ref[at, :]
                ref, place = pick(logits, at)
                acc[:, lanes] += jnp.sum((scaled * ref[place, lanes]).reshape(folded), axis=0)
            ref, place = pick(lg_ref, at)
            logits = ref[place, lanes]
            scaled = e_ref[at, lanes] * cs_ref[at, :]
            powers = jnp.exp(logits).reshape(folded) * rows[0:8, lanes][None]
            target = scaled.reshape(folded) * rows[8:16, lanes][None]
            g[at, lanes] = (powers - target).reshape(logits.shape).astype(BF16)

    def matmuls(lanes):
        db_ref[lanes, :] = jnp.dot(cols_ref[...], g[:, lanes], preferred_element_type=F32).T
        if lanes.stop % DEPTH == 0:
            deep = slice(lanes.stop - DEPTH, lanes.stop)
            if last is not None and lanes.stop == half:
                for at in chunks(protos, CHUNK):
                    term = lax.dot_general(turned_ref[:, deep], g[at, deep], NT, preferred_element_type=F32)
                    last(at, unit_sum[:, at] + term)
                return
            term = lax.dot_general(turned_ref[:, deep], g[:, deep], NT, preferred_element_type=F32)
            if lanes.stop > DEPTH:
                unit_sum[...] += term
            else:
                unit_sum[...] = term if start is None else start[...] + term

    before = None
    for lanes in chunks(half, CHUNK):
        elementwise(lanes)
        if before is not None:
            matmuls(before)
        before = lanes
    matmuls(before)


def grad_other_kernel(
    devices, e_ref, lg_other, cs_ref, cols_ref, turned_ref, mine_ref, theirs_ref, base_ref, e_own, lg_own_a, lg_own_b,
    db_ref, unit_sum, loss_ref, g, rows, acc, acc_own
):
    row = flat(theirs_ref[0:4, :] + base_ref[4:8, :])
    part = flat(theirs_ref[4:8, :])
    lg_ref = (lg_other,)
    cross = ((e_ref, lg_ref, acc), (e_own, (lg_own_a, lg_own_b), acc_own))
    half_gradients(row, part, e_ref, lg_ref, cs_ref, cols_ref, turned_ref, db_ref, unit_sum, None, g, rows, cross)
    parts = jnp.log(part) + jnp.log(flat(mine_ref[4:8, :]))
    row_own = flat(mine_ref[0:4, :] + base_ref[0:4, :])
    crossed = jnp.sum(acc[...], axis=0, keepdims=True) / row + jnp.sum(acc_own[...], axis=0, keepdims=True) / row_own
    terms = parts * (1.0 / devices) - crossed
    loss_ref[...] = sum(terms[:, lanes] for lanes in chunks(terms.shape[1], loss_ref.shape[1]))
    db_ref[e_ref.shape[1] :, :] = jnp.broadcast_to(loss_ref[...], (8, loss_ref.shape[1]))


def grad_own_kernel(
    e_ref, lg_a, lg_b, cs_ref, cols_ref, turned_ref, mine_ref, base_ref, other_sum, w_ref,
    db_ref, dp_ref, g, rows, unit_sum, out_buf, sem
):
    row = flat(mine_ref[0:4, :] + base_ref[0:4, :])
    part = flat(mine_ref[4:8, :])
    lg_ref = (lg_a, lg_b)
    copies = []

    def project(at, d_unit):
        unit, inv = columns(w_ref[:, at])
        out_buf[:, at] = inv * (d_unit - unit * jnp.sum(unit * d_unit, axis=0, keepdims=True))
        j = len(copies)
        copies.append(pltpu.make_async_copy(out_buf.at[:, at], dp_ref.at[:, at], sem.at[j]))
        copies[j].start()

    half_gradients(
        row, part, e_ref, lg_ref, cs_ref, cols_ref, turned_ref, db_ref, unit_sum, other_sum, g, rows, (), project
    )
    for copy in copies:
        copy.wait()


def parts_of(value):
    high = value.astype(BF16).astype(F32)
    mid = (value - high).astype(BF16).astype(F32)
    return high, mid, value - high - mid


def pack_kernel(mine_ref, theirs_ref, loss_ref, s_ref, out_ref):
    rows = mine_ref.shape[0]
    lane = lax.broadcasted_iota(jnp.int32, (8, 128), 1)
    total = jnp.sum(loss_ref[...] + theirs_ref[rows : rows + 1, :], axis=1, keepdims=True)
    loss = jnp.zeros((8, 128), F32)
    for j, part in enumerate(parts_of(total)):
        loss = jnp.where(lane == 9 + j, part, loss)

    group = 8

    def step(i, _):
        at = pl.ds(pl.multiple_of(i * 24 * group, 8), 24 * group)
        block = mine_ref[at, :] + theirs_ref[at, :]
        unit = s_ref[pl.ds(i * group, group)].astype(F32).reshape(block.shape)
        along = jnp.sum(block * unit, axis=1, keepdims=True)
        block = (block - unit * along).astype(BF16).reshape(group, 24, block.shape[1])
        parts = [part.reshape(group, 24, 1) for part in parts_of(along)]
        tail = jnp.broadcast_to(loss[None], (group, 8, 128))
        for j, part in enumerate(parts):
            for k in range(3):
                tail = jnp.where((lane == 3 * j + k)[None], part[:, 8 * k : 8 * (k + 1), :], tail)
        chips = pl.ds(i * group, group)
        for k in range(3):
            out_ref[chips, 24 * k : 24 * (k + 1), :] = block[:, :, 128 * k : 128 * (k + 1)]
        out_ref[chips, 72:80, :] = tail.astype(BF16)
        return 0

    lax.fori_loop(0, out_ref.shape[0] // group, step, 0, unroll=2)


def finish_kernel(images, got_ref, hid_ref, ds_ref, loss_ref):
    total = jnp.sum(got_ref[...].astype(F32), axis=0)
    tail = total[72:80, :]
    along = jnp.concatenate([tail[:, k : k + 1] + tail[:, 3 + k : 4 + k] + tail[:, 6 + k : 7 + k] for k in range(3)], axis=0)
    wide = hid_ref[...].astype(F32)
    inv = lax.rsqrt(jnp.sum(wide * wide, axis=1, keepdims=True) + EPS)
    unit = wide * inv
    d_bot = jnp.concatenate([total[24 * k : 24 * (k + 1), :] for k in range(3)], axis=1)
    d_bot = d_bot + unit.astype(BF16).astype(F32) * along
    ds_ref[...] = inv * (d_bot - unit * jnp.sum(unit * d_bot, axis=1, keepdims=True))
    loss = tail[0:1, 9:10] + tail[0:1, 10:11] + tail[0:1, 11:12]
    loss_ref[...] = jnp.broadcast_to(loss * (1.0 / images), loss_ref.shape)


def body(teacher_hidden, teacher_proj, student_hidden, teacher_protos, student_protos):
    chips = lax.axis_size(CHIPS)
    rows_dev, bot = student_hidden.shape
    half = rows_dev * chips
    images = 2 * half
    protos = teacher_protos.shape[1]
    total_cols = protos * lax.axis_size(ALL)
    sds = jax.ShapeDtypeStruct

    def swap(x):
        return lax.ppermute(x, "c", SWAP)

    def exchange(x):
        return lax.all_to_all(x, CHIPS, 0, 0)

    def row_sums(x, rows):
        mine = call(sum_kernel, sds((rows, images // 8), F32), (exchange(x),), 2)
        return mine, swap(mine)

    t_send, s_bot = call(
        rows_kernel,
        (sds((chips, rows_dev, bot), BF16), sds((rows_dev, bot), BF16)),
        (student_hidden, teacher_hidden, teacher_proj),
        60,
        [
            pltpu.VMEM(student_hidden.shape, BF16),
            pltpu.VMEM(teacher_hidden.shape, BF16),
            pltpu.VMEM((2, teacher_proj.shape[0] // 2, bot), BF16),
            pltpu.SemaphoreType.DMA((4,)),
        ],
        in_any=(0, 1, 2),
    )
    t_own = exchange(t_send).reshape(half, bot)
    t_other = swap(t_own)

    matrix = sds((protos, half), F32)
    lhs = sds((protos, bot), BF16)
    column = sds((protos, 1), F32)
    turned = sds((bot, half), BF16)
    vec8 = sds((8, images // 8), F32)
    vec4 = sds((4, images // 8), F32)
    send8 = sds((chips, 8, images // 8), BF16)
    fold8 = pltpu.VMEM((8, images), F32)
    half_acc = pltpu.VMEM((8, half), F32)
    scales = pltpu.VMEM((protos, 1), F32)

    e_own, t_lhs, sums = call(teacher_own_kernel, (matrix, lhs, column), (teacher_protos, t_own), 8)
    sums, student_late = lax.optimization_barrier((sums, student_protos))
    s_lhs, s_cols = call(student_columns_kernel, (lhs, sds((bot, protos), BF16)), (student_late,), 8)
    t_other, s_lhs, s_cols = lax.optimization_barrier((t_other, s_lhs, s_cols))
    e_other, sent = call(
        functools.partial(teacher_other_kernel, total_cols, 1.0 / (2 * chips * images)),
        (matrix, sds((chips, 8 + rows_dev, bot), BF16)),
        (t_lhs, t_other, e_own, sums, s_bot),
        8,
        [fold8],
    )
    mine, s_own = call(open_kernel, (vec8, sds((chips, rows_dev, bot), BF16)), (exchange(sent),), 4)
    theirs = swap(mine)
    s_own = s_own.reshape(half, bot)

    def student(start, stop, rows):
        shapes = (sds((stop - start, half), F32), vec4)
        return call(functools.partial(student_kernel, start), shapes, (s_lhs, rows), 8, [half_acc])

    split = protos * 3 // 4
    lg_own_a, part_own = student(0, split, s_own)
    theirs, part_own, s_late = lax.optimization_barrier((theirs, part_own, s_own))
    s_other = swap(s_late)
    one_pass = functools.partial(pass_kernel, total_cols, images, 2 * chips)
    sent, before = call(
        one_pass,
        (send8, vec8),
        (e_own, e_other, mine, theirs),
        4,
        [scales, fold8, fold8],
    )
    mine, theirs = row_sums(sent, 8)
    late, s_late = lax.optimization_barrier((mine, s_other))
    lg_other, part_other = student(0, protos, s_late)
    theirs, part_other = lax.optimization_barrier((theirs, part_other))
    row, before, col_scale = call(
        one_pass,
        (vec8, vec8, column),
        (e_own, e_other, late, theirs, before),
        4,
        [fold8, fold8],
    )
    pair_other = call(pair_kernel, vec8, (row, part_other), 2)
    pair_theirs = swap(pair_other)
    pair_other, own_late = lax.optimization_barrier((pair_other, s_own))
    lg_own_b, part_own_rest = student(split, protos, own_late)
    pair_theirs, part_own_rest = lax.optimization_barrier((pair_theirs, part_own_rest))
    mine, theirs = row_sums(call(send_kernel, send8, (row, part_own, part_own_rest, pair_theirs), 2), 8)
    mine, own_late, other_late = lax.optimization_barrier((mine, s_own, s_other))
    turned_own = call(turn_kernel, turned, (own_late,), 2)
    turned_other = call(turn_kernel, turned, (other_late,), 2)
    theirs, turned_own, turned_other = lax.optimization_barrier((theirs, turned_own, turned_other))
    tile = sds((1, bot), F32)
    grads = [pltpu.VMEM((protos, half), BF16), pltpu.VMEM((16, half), F32)]
    d_other, unit_sum, loss_mine = call(
        functools.partial(grad_other_kernel, 2 * chips),
        (sds((half + 8, bot), F32), sds((bot, protos), F32), tile),
        (e_other, lg_other, col_scale, s_cols, turned_other, mine, theirs, before, e_own, lg_own_a, lg_own_b),
        8,
        grads + [half_acc, half_acc],
    )
    d_theirs = swap(d_other)
    whole = pltpu.VMEM((bot, protos), F32)
    d_mine, d_protos = call(
        grad_own_kernel,
        (sds((half, bot), F32), sds((bot, protos), F32)),
        (e_own, lg_own_a, lg_own_b, col_scale, s_cols, turned_own, mine, before, unit_sum, student_protos),
        12,
        grads + [whole, whole, pltpu.SemaphoreType.DMA((protos // CHUNK,))],
        out_any=(1,),
    )
    packed = call(
        pack_kernel,
        sds((chips, 80, 128), BF16),
        (d_mine, d_theirs, loss_mine, s_own.reshape(chips, rows_dev, bot)),
        4,
    )
    got = exchange(packed)
    d_student, loss = call(
        functools.partial(finish_kernel, images),
        (sds((rows_dev, bot), F32), sds((1, 128), F32)),
        (got, student_hidden),
        4,
    )
    return loss[0, 0], d_student, d_protos


def solution(mesh):
    grid = Mesh(mesh.devices.reshape(4, 4, 4, 2), ALL)
    return jax.shard_map(
        body,
        mesh=grid,
        in_specs=(P(ALL, None), P(), P(ALL, None), P(None, ALL), P(None, ALL)),
        out_specs=(P(), P(ALL, None), P(None, ALL)),
        check_vma=False,
    )
```

```python
import functools

import jax
import jax.numpy as jnp
from jax import lax
from jax.experimental import pallas as pl
from jax.experimental.pallas import tpu as pltpu
from jax.sharding import Mesh
from jax.sharding import PartitionSpec as P

ITERS = 3
EPS = 1e-06
teacher_temp = 0.07
student_temp = 0.1

ALL = ("z", "y", "x", "c")
CHIPS = ("x", "y", "z")
SWAP = [(0, 1), (1, 0)]
F32 = jnp.float32
BF16 = jnp.bfloat16
MB = 1024 * 1024
NT = (((1,), (1,)), ((), ()))
VM = pl.BlockSpec(memory_space=pltpu.VMEM)
CHUNK = 256
BLOCK = 256
ANY = pl.BlockSpec(memory_space=pltpu.HBM)


def call(kernel, out_shape, operands, vmem, scratch=(), in_any=(), out_any=(), flops=0, nbytes=0):
    many = isinstance(out_shape, (tuple, list))
    outs = out_shape if many else (out_shape,)
    specs = tuple(ANY if i in out_any else VM for i in range(len(outs)))
    return pl.pallas_call(
        kernel,
        out_shape=out_shape,
        in_specs=[ANY if i in in_any else VM for i in range(len(operands))],
        out_specs=specs if many else specs[0],
        scratch_shapes=list(scratch),
        compiler_params=pltpu.CompilerParams(vmem_limit_bytes=vmem * MB),
        cost_estimate=pl.CostEstimate(flops=flops, bytes_accessed=nbytes, transcendentals=0),
    )(*operands)


def fold(row):
    width = row.shape[1] // 8
    return jnp.concatenate([row[:, j * width : (j + 1) * width] for j in range(8)], axis=0)


def spread(piece, ref):
    piece = piece.astype(ref.dtype)
    for i in range(ref.shape[0]):
        ref[i] = piece


def flat(block):
    return jnp.concatenate([block[j : j + 1, :] for j in range(block.shape[0])], axis=1)


def total_row(mine, theirs):
    return flat(mine + jnp.concatenate([theirs[4:8, :], theirs[0:4, :]], axis=0))


def columns(w_block):
    wide = w_block.astype(F32)
    inv = lax.rsqrt(jnp.sum(wide * wide, axis=0, keepdims=True) + EPS)
    return wide * inv, inv


def rows_kernel(s_ref, hid_ref, proj_ref, send_ref, s_out_ref, s_buf, hid_buf, proj_buf, sem):
    parts = proj_buf.shape[0]
    depth = proj_buf.shape[1]
    first = pltpu.make_async_copy(s_ref, s_buf, sem.at[0])
    second = pltpu.make_async_copy(hid_ref, hid_buf, sem.at[1])
    copies = [
        pltpu.make_async_copy(proj_ref.at[pl.ds(i * depth, depth), :], proj_buf.at[i], sem.at[2 + i])
        for i in range(parts)
    ]
    first.start()
    second.start()
    for copy in copies:
        copy.start()
    first.wait()
    wide = s_buf[...].astype(F32)
    unit = wide * lax.rsqrt(jnp.sum(wide * wide, axis=1, keepdims=True) + EPS)
    s_out_ref[...] = unit.astype(BF16)
    second.wait()
    t_hid = jnp.zeros((hid_buf.shape[0], proj_buf.shape[2]), F32)
    for i, copy in enumerate(copies):
        copy.wait()
        t_hid = t_hid + jnp.dot(
            hid_buf[:, i * depth : (i + 1) * depth], proj_buf[i], preferred_element_type=F32
        )
    t_bot = t_hid * lax.rsqrt(jnp.sum(t_hid * t_hid, axis=1, keepdims=True) + EPS)
    spread(t_bot, send_ref)


def sum_kernel(got_ref, out_ref):
    out_ref[...] = jnp.sum(got_ref[...].astype(F32), axis=0)


def chunks(total, size):
    return [slice(j, j + size) for j in range(0, total, size)]


def expo_block(at, lhs_ref, rows_ref, e_ref):
    prod = lax.dot_general(lhs_ref[at, :], rows_ref[...], NT, preferred_element_type=F32)
    expo = jnp.exp(prod * (1.0 / teacher_temp))
    e_ref[at, :] = expo
    return jnp.sum(expo, axis=1, keepdims=True)


def teacher_own_kernel(w_ref, rows_ref, e_ref, lhs_ref, sums_ref):
    for at in chunks(w_ref.shape[1], CHUNK):
        lhs_ref[at, :] = columns(w_ref[:, at])[0].T.astype(BF16)
        sums_ref[at, :] = expo_block(at, lhs_ref, rows_ref, e_ref)


def teacher_other_kernel(total_cols, expected, lhs_ref, rows_ref, e_own, sums_ref, s_ref, e_ref, out_ref, acc):
    half = rows_ref.shape[0]
    acc[...] = jnp.zeros_like(acc)
    for at in chunks(lhs_ref.shape[0], CHUNK):
        scale = 1.0 / (total_cols * (sums_ref[at, :] + expo_block(at, lhs_ref, rows_ref, e_ref)))
        row_pass(e_own.at[at, :], scale, acc.at[:, :half])
        row_pass(e_ref.at[at, :], scale, acc.at[:, half:])
    sums = fold(jnp.sum(acc[...], axis=0, keepdims=True)) - expected
    spread(jnp.concatenate([sums, s_ref[...].astype(F32)], axis=0), out_ref)


def open_kernel(got_ref, sums_ref, rows_ref):
    total = jnp.zeros(sums_ref.shape, F32)
    for i in range(got_ref.shape[0]):
        piece = got_ref[i].astype(F32)
        total = total + piece[0:8, :]
        rows_ref[i] = piece[8:, :].astype(BF16)
    sums_ref[...] = total


def fold_half(part):
    row = jnp.sum(part, axis=0, keepdims=True)
    width = row.shape[1] // 4
    return jnp.concatenate([row[:, j * width : (j + 1) * width] for j in range(4)], axis=0)


def student_columns_kernel(w_ref, lhs_ref, cols_ref):
    for at in chunks(w_ref.shape[1], CHUNK):
        unit = columns(w_ref[:, at])[0]
        cols_ref[:, at] = unit.astype(BF16)
        lhs_ref[at, :] = unit.T.astype(BF16)


def student_kernel(start, lhs_ref, rows_ref, lg_ref, out_ref, part):
    part[...] = jnp.zeros_like(part)
    for at in chunks(lg_ref.shape[0], CHUNK):
        lhs = lhs_ref[start + at.start : start + at.stop, :]
        prod = lax.dot_general(lhs, rows_ref[...], NT, preferred_element_type=F32)
        logits = prod * (1.0 / student_temp)
        lg_ref[at, :] = logits
        part[...] += jnp.sum(jnp.exp(logits).reshape(CHUNK // 8, 8, logits.shape[1]), axis=0)
    out_ref[...] = fold_half(part[...])


def pair_kernel(row_ref, part_ref, out_ref):
    out_ref[...] = jnp.concatenate([row_ref[4:8, :], part_ref[...]], axis=0)


def send_kernel(row_ref, part_a, part_b, theirs_ref, out_ref):
    spread(jnp.concatenate([row_ref[0:4, :], part_a[...] + part_b[...]], axis=0) + theirs_ref[...], out_ref)


def pick(refs, at):
    if len(refs) == 1:
        return refs[0], at
    first = refs[0].shape[0]
    if at.stop <= first:
        return refs[0], at
    return refs[1], slice(at.start - first, at.stop - first)


def turn_kernel(rows_ref, out_ref):
    out_ref[...] = rows_ref[...].T


def row_pass(block_ref, scale, acc):
    rows, n = block_ref.shape
    scale = scale.reshape(rows // 8, 8, 1)
    for start in range(0, n, 512):
        lanes = slice(start, start + 512)
        acc[:, lanes] += jnp.sum(block_ref[:, lanes].reshape(rows // 8, 8, 512) * scale, axis=0)


def pass_kernel(total_cols, images, devices, own_ref, other_ref, mine_ref, theirs_ref, *rest):
    *before, out_ref, total_ref, cs_ref, weight, acc = rest
    total = total_row(mine_ref[...], theirs_ref[...])
    total = total + (flat(before[0][...]) if before else 1.0 / images)
    total_ref[...] = fold(total)
    weight[...] = jnp.broadcast_to(1.0 / (images * total), weight.shape)
    acc[...] = jnp.zeros_like(acc)
    protos, half = own_ref.shape

    def step(j, _):
        at = pl.ds(pl.multiple_of(j * BLOCK, BLOCK), BLOCK)
        sums = jnp.zeros((BLOCK, 1), F32)
        for ref, start in ((own_ref, 0), (other_ref, half)):
            weighted = ref[at, :].reshape(BLOCK // 8, 8, half) * weight[:, start : start + half][None]
            sums = sums + jnp.sum(weighted.reshape(BLOCK, half), axis=1, keepdims=True)
        scale = 1.0 / (total_cols * sums)
        cs_ref[at, :] = scale
        row_pass(own_ref.at[at, :], scale, acc.at[:, :half])
        row_pass(other_ref.at[at, :], scale, acc.at[:, half:])
        return 0

    lax.fori_loop(0, protos // BLOCK, step, 0)
    piece = fold(jnp.sum(acc[...], axis=0, keepdims=True)) - total_ref[...] * (1.0 / devices)
    if len(out_ref.shape) == 3:
        spread(piece, out_ref)
    else:
        out_ref[...] = piece


STRIP = 32
DEPTH = 512


def half_gradients(
    row, part, e_ref, lg_ref, cs_ref, cols_ref, turned_ref, db_ref, unit_sum, start, g, rows, cross, last=None
):
    protos, half = e_ref.shape
    rows[0:8, :] = jnp.broadcast_to((1.0 / student_temp) / part, (8, half))
    rows[8:16, :] = jnp.broadcast_to((1.0 / student_temp) / row, (8, half))
    folded = (STRIP // 8, 8, CHUNK)
    for _, _, acc in cross:
        acc[...] = jnp.zeros_like(acc)

    def elementwise(lanes):
        for at in chunks(protos, STRIP):
            for expo, logits, acc in cross:
                scaled = expo[at, lanes] * cs_ref[at, :]
                ref, place = pick(logits, at)
                acc[:, lanes] += jnp.sum((scaled * ref[place, lanes]).reshape(folded), axis=0)
            ref, place = pick(lg_ref, at)
            logits = ref[place, lanes]
            scaled = e_ref[at, lanes] * cs_ref[at, :]
            powers = jnp.exp(logits).reshape(folded) * rows[0:8, lanes][None]
            target = scaled.reshape(folded) * rows[8:16, lanes][None]
            g[at, lanes] = (powers - target).reshape(logits.shape).astype(BF16)

    def matmuls(lanes):
        db_ref[lanes, :] = jnp.dot(cols_ref[...], g[:, lanes], preferred_element_type=F32).T
        if lanes.stop % DEPTH == 0:
            deep = slice(lanes.stop - DEPTH, lanes.stop)
            if last is not None and lanes.stop == half:
                for at in chunks(protos, CHUNK):
                    term = lax.dot_general(turned_ref[:, deep], g[at, deep], NT, preferred_element_type=F32)
                    last(at, unit_sum[:, at] + term)
                return
            term = lax.dot_general(turned_ref[:, deep], g[:, deep], NT, preferred_element_type=F32)
            if lanes.stop > DEPTH:
                unit_sum[...] += term
            else:
                unit_sum[...] = term if start is None else start[...] + term

    before = None
    for lanes in chunks(half, CHUNK):
        elementwise(lanes)
        if before is not None:
            matmuls(before)
        before = lanes
    matmuls(before)


def grad_other_kernel(
    devices, e_ref, lg_other, cs_ref, cols_ref, turned_ref, mine_ref, theirs_ref, base_ref, e_own, lg_own_a, lg_own_b,
    db_ref, unit_sum, loss_ref, g, rows, acc, acc_own
):
    row = flat(theirs_ref[0:4, :] + base_ref[4:8, :])
    part = flat(theirs_ref[4:8, :])
    lg_ref = (lg_other,)
    cross = ((e_ref, lg_ref, acc), (e_own, (lg_own_a, lg_own_b), acc_own))
    half_gradients(row, part, e_ref, lg_ref, cs_ref, cols_ref, turned_ref, db_ref, unit_sum, None, g, rows, cross)
    parts = jnp.log(part) + jnp.log(flat(mine_ref[4:8, :]))
    row_own = flat(mine_ref[0:4, :] + base_ref[0:4, :])
    crossed = jnp.sum(acc[...], axis=0, keepdims=True) / row + jnp.sum(acc_own[...], axis=0, keepdims=True) / row_own
    terms = parts * (1.0 / devices) - crossed
    loss_ref[...] = sum(terms[:, lanes] for lanes in chunks(terms.shape[1], loss_ref.shape[1]))
    db_ref[e_ref.shape[1] :, :] = jnp.broadcast_to(loss_ref[...], (8, loss_ref.shape[1]))


def grad_own_kernel(
    e_ref, lg_a, lg_b, cs_ref, cols_ref, turned_ref, mine_ref, base_ref, other_sum, w_ref,
    db_ref, dp_ref, g, rows, unit_sum, out_buf, sem
):
    row = flat(mine_ref[0:4, :] + base_ref[0:4, :])
    part = flat(mine_ref[4:8, :])
    lg_ref = (lg_a, lg_b)
    copies = []

    def project(at, d_unit):
        unit, inv = columns(w_ref[:, at])
        out_buf[:, at] = inv * (d_unit - unit * jnp.sum(unit * d_unit, axis=0, keepdims=True))
        j = len(copies)
        copies.append(pltpu.make_async_copy(out_buf.at[:, at], dp_ref.at[:, at], sem.at[j]))
        copies[j].start()

    half_gradients(
        row, part, e_ref, lg_ref, cs_ref, cols_ref, turned_ref, db_ref, unit_sum, other_sum, g, rows, (), project
    )
    for copy in copies:
        copy.wait()


def parts_of(value):
    high = value.astype(BF16).astype(F32)
    mid = (value - high).astype(BF16).astype(F32)
    return high, mid, value - high - mid


def pack_kernel(mine_ref, theirs_ref, loss_ref, s_ref, out_ref):
    rows = mine_ref.shape[0]
    lane = lax.broadcasted_iota(jnp.int32, (8, 128), 1)
    total = jnp.sum(loss_ref[...] + theirs_ref[rows : rows + 1, :], axis=1, keepdims=True)
    loss = jnp.zeros((8, 128), F32)
    for j, part in enumerate(parts_of(total)):
        loss = jnp.where(lane == 9 + j, part, loss)

    group = 8

    def step(i, _):
        at = pl.ds(pl.multiple_of(i * 24 * group, 8), 24 * group)
        block = mine_ref[at, :] + theirs_ref[at, :]
        unit = s_ref[pl.ds(i * group, group)].astype(F32).reshape(block.shape)
        along = jnp.sum(block * unit, axis=1, keepdims=True)
        block = (block - unit * along).astype(BF16).reshape(group, 24, block.shape[1])
        parts = [part.reshape(group, 24, 1) for part in parts_of(along)]
        tail = jnp.broadcast_to(loss[None], (group, 8, 128))
        for j, part in enumerate(parts):
            for k in range(3):
                tail = jnp.where((lane == 3 * j + k)[None], part[:, 8 * k : 8 * (k + 1), :], tail)
        chips = pl.ds(i * group, group)
        for k in range(3):
            out_ref[chips, 24 * k : 24 * (k + 1), :] = block[:, :, 128 * k : 128 * (k + 1)]
        out_ref[chips, 72:80, :] = tail.astype(BF16)
        return 0

    lax.fori_loop(0, out_ref.shape[0] // group, step, 0, unroll=2)


def finish_kernel(images, got_ref, hid_ref, ds_ref, loss_ref):
    total = jnp.sum(got_ref[...].astype(F32), axis=0)
    tail = total[72:80, :]
    along = jnp.concatenate([tail[:, k : k + 1] + tail[:, 3 + k : 4 + k] + tail[:, 6 + k : 7 + k] for k in range(3)], axis=0)
    wide = hid_ref[...].astype(F32)
    inv = lax.rsqrt(jnp.sum(wide * wide, axis=1, keepdims=True) + EPS)
    unit = wide * inv
    d_bot = jnp.concatenate([total[24 * k : 24 * (k + 1), :] for k in range(3)], axis=1)
    d_bot = d_bot + unit.astype(BF16).astype(F32) * along
    ds_ref[...] = inv * (d_bot - unit * jnp.sum(unit * d_bot, axis=1, keepdims=True))
    loss = tail[0:1, 9:10] + tail[0:1, 10:11] + tail[0:1, 11:12]
    loss_ref[...] = jnp.broadcast_to(loss * (1.0 / images), loss_ref.shape)


def body(teacher_hidden, teacher_proj, student_hidden, teacher_protos, student_protos):
    chips = lax.axis_size(CHIPS)
    rows_dev, bot = student_hidden.shape
    half = rows_dev * chips
    images = 2 * half
    protos = teacher_protos.shape[1]
    total_cols = protos * lax.axis_size(ALL)
    sds = jax.ShapeDtypeStruct

    def swap(x):
        return lax.ppermute(x, "c", SWAP)

    def exchange(x):
        return lax.all_to_all(x, CHIPS, 0, 0)

    def row_sums(x, rows):
        mine = call(sum_kernel, sds((rows, images // 8), F32), (exchange(x),), 2)
        return mine, swap(mine)

    t_send, s_bot = call(
        rows_kernel,
        (sds((chips, rows_dev, bot), BF16), sds((rows_dev, bot), BF16)),
        (student_hidden, teacher_hidden, teacher_proj),
        60,
        [
            pltpu.VMEM(student_hidden.shape, BF16),
            pltpu.VMEM(teacher_hidden.shape, BF16),
            pltpu.VMEM((2, teacher_proj.shape[0] // 2, bot), BF16),
            pltpu.SemaphoreType.DMA((4,)),
        ],
        in_any=(0, 1, 2),
    )
    t_own = exchange(t_send).reshape(half, bot)
    t_other = swap(t_own)

    matrix = sds((protos, half), F32)
    lhs = sds((protos, bot), BF16)
    column = sds((protos, 1), F32)
    turned = sds((bot, half), BF16)
    vec8 = sds((8, images // 8), F32)
    vec4 = sds((4, images // 8), F32)
    send8 = sds((chips, 8, images // 8), BF16)
    fold8 = pltpu.VMEM((8, images), F32)
    half_acc = pltpu.VMEM((8, half), F32)
    scales = pltpu.VMEM((protos, 1), F32)

    e_own, t_lhs, sums = call(teacher_own_kernel, (matrix, lhs, column), (teacher_protos, t_own), 8)
    sums, student_late = lax.optimization_barrier((sums, student_protos))
    s_lhs, s_cols = call(student_columns_kernel, (lhs, sds((bot, protos), BF16)), (student_late,), 8)
    t_other, s_lhs, s_cols = lax.optimization_barrier((t_other, s_lhs, s_cols))
    e_other, sent = call(
        functools.partial(teacher_other_kernel, total_cols, 1.0 / (2 * chips * images)),
        (matrix, sds((chips, 8 + rows_dev, bot), BF16)),
        (t_lhs, t_other, e_own, sums, s_bot),
        8,
        [fold8],
    )
    mine, s_own = call(open_kernel, (vec8, sds((chips, rows_dev, bot), BF16)), (exchange(sent),), 4)
    theirs = swap(mine)
    s_own = s_own.reshape(half, bot)

    def student(start, stop, rows):
        shapes = (sds((stop - start, half), F32), vec4)
        return call(functools.partial(student_kernel, start), shapes, (s_lhs, rows), 8, [half_acc])

    split = protos * 3 // 4
    lg_own_a, part_own = student(0, split, s_own)
    theirs, part_own, s_late = lax.optimization_barrier((theirs, part_own, s_own))
    s_other = swap(s_late)
    one_pass = functools.partial(pass_kernel, total_cols, images, 2 * chips)
    sent, before = call(
        one_pass,
        (send8, vec8),
        (e_own, e_other, mine, theirs),
        4,
        [scales, fold8, fold8],
    )
    mine, theirs = row_sums(sent, 8)
    late, s_late = lax.optimization_barrier((mine, s_other))
    lg_other, part_other = student(0, protos, s_late)
    theirs, part_other = lax.optimization_barrier((theirs, part_other))
    row, before, col_scale = call(
        one_pass,
        (vec8, vec8, column),
        (e_own, e_other, late, theirs, before),
        4,
        [fold8, fold8],
    )
    pair_other = call(pair_kernel, vec8, (row, part_other), 2)
    pair_theirs = swap(pair_other)
    pair_other, own_late = lax.optimization_barrier((pair_other, s_own))
    lg_own_b, part_own_rest = student(split, protos, own_late)
    pair_theirs, part_own_rest = lax.optimization_barrier((pair_theirs, part_own_rest))
    mine, theirs = row_sums(call(send_kernel, send8, (row, part_own, part_own_rest, pair_theirs), 2), 8)
    mine, own_late, other_late = lax.optimization_barrier((mine, s_own, s_other))
    turned_own = call(turn_kernel, turned, (own_late,), 2)
    turned_other = call(turn_kernel, turned, (other_late,), 2)
    theirs, turned_own, turned_other = lax.optimization_barrier((theirs, turned_own, turned_other))
    tile = sds((1, bot), F32)
    grads = [pltpu.VMEM((protos, half), BF16), pltpu.VMEM((16, half), F32)]
    d_other, unit_sum, loss_mine = call(
        functools.partial(grad_other_kernel, 2 * chips),
        (sds((half + 8, bot), F32), sds((bot, protos), F32), tile),
        (e_other, lg_other, col_scale, s_cols, turned_other, mine, theirs, before, e_own, lg_own_a, lg_own_b),
        8,
        grads + [half_acc, half_acc],
    )
    d_theirs = swap(d_other)
    whole = pltpu.VMEM((bot, protos), F32)
    d_mine, d_protos = call(
        grad_own_kernel,
        (sds((half, bot), F32), sds((bot, protos), F32)),
        (e_own, lg_own_a, lg_own_b, col_scale, s_cols, turned_own, mine, before, unit_sum, student_protos),
        12,
        grads + [whole, whole, pltpu.SemaphoreType.DMA((protos // CHUNK,))],
        out_any=(1,),
    )
    packed = call(
        pack_kernel,
        sds((chips, 80, 128), BF16),
        (d_mine, d_theirs, loss_mine, s_own.reshape(chips, rows_dev, bot)),
        4,
    )
    got = exchange(packed)
    d_student, loss = call(
        functools.partial(finish_kernel, images),
        (sds((rows_dev, bot), F32), sds((1, 128), F32)),
        (got, student_hidden),
        4,
    )
    return loss[0, 0], d_student, d_protos


def solution(mesh):
    grid = Mesh(mesh.devices.reshape(4, 4, 4, 2), ALL)
    return jax.shard_map(
        body,
        mesh=grid,
        in_specs=(P(ALL, None), P(), P(ALL, None), P(None, ALL), P(None, ALL)),
        out_specs=(P(), P(ALL, None), P(None, ALL)),
        check_vma=False,
    )
```

```python
import functools

import jax
import jax.numpy as jnp
from jax import lax
from jax.experimental import pallas as pl
from jax.experimental.pallas import tpu as pltpu
from jax.sharding import Mesh
from jax.sharding import PartitionSpec as P

ITERS = 3
EPS = 1e-06
teacher_temp = 0.07
student_temp = 0.1

ALL = ("z", "y", "x", "c")
CHIPS = ("x", "y", "z")
SWAP = [(0, 1), (1, 0)]
F32 = jnp.float32
BF16 = jnp.bfloat16
MB = 1024 * 1024
NT = (((1,), (1,)), ((), ()))
VM = pl.BlockSpec(memory_space=pltpu.VMEM)
CHUNK = 256
BLOCK = 256
ANY = pl.BlockSpec(memory_space=pltpu.HBM)


def call(kernel, out_shape, operands, vmem, scratch=(), in_any=(), out_any=(), flops=0, nbytes=0):
    many = isinstance(out_shape, (tuple, list))
    outs = out_shape if many else (out_shape,)
    specs = tuple(ANY if i in out_any else VM for i in range(len(outs)))
    return pl.pallas_call(
        kernel,
        out_shape=out_shape,
        in_specs=[ANY if i in in_any else VM for i in range(len(operands))],
        out_specs=specs if many else specs[0],
        scratch_shapes=list(scratch),
        compiler_params=pltpu.CompilerParams(vmem_limit_bytes=vmem * MB),
        cost_estimate=pl.CostEstimate(flops=flops, bytes_accessed=nbytes, transcendentals=0),
    )(*operands)


def fold(row):
    width = row.shape[1] // 8
    return jnp.concatenate([row[:, j * width : (j + 1) * width] for j in range(8)], axis=0)


def spread(piece, ref):
    piece = piece.astype(ref.dtype)
    for i in range(ref.shape[0]):
        ref[i] = piece


def flat(block):
    return jnp.concatenate([block[j : j + 1, :] for j in range(block.shape[0])], axis=1)


def total_row(mine, theirs):
    return flat(mine + jnp.concatenate([theirs[4:8, :], theirs[0:4, :]], axis=0))


def columns(w_block):
    wide = w_block.astype(F32)
    inv = lax.rsqrt(jnp.sum(wide * wide, axis=0, keepdims=True) + EPS)
    return wide * inv, inv


def rows_kernel(s_ref, hid_ref, proj_ref, send_ref, s_out_ref, s_buf, hid_buf, proj_buf, sem):
    parts = proj_buf.shape[0]
    depth = proj_buf.shape[1]
    first = pltpu.make_async_copy(s_ref, s_buf, sem.at[0])
    second = pltpu.make_async_copy(hid_ref, hid_buf, sem.at[1])
    copies = [
        pltpu.make_async_copy(proj_ref.at[pl.ds(i * depth, depth), :], proj_buf.at[i], sem.at[2 + i])
        for i in range(parts)
    ]
    first.start()
    second.start()
    for copy in copies:
        copy.start()
    first.wait()
    wide = s_buf[...].astype(F32)
    unit = wide * lax.rsqrt(jnp.sum(wide * wide, axis=1, keepdims=True) + EPS)
    s_out_ref[...] = unit.astype(BF16)
    second.wait()
    t_hid = jnp.zeros((hid_buf.shape[0], proj_buf.shape[2]), F32)
    for i, copy in enumerate(copies):
        copy.wait()
        t_hid = t_hid + jnp.dot(
            hid_buf[:, i * depth : (i + 1) * depth], proj_buf[i], preferred_element_type=F32
        )
    t_bot = t_hid * lax.rsqrt(jnp.sum(t_hid * t_hid, axis=1, keepdims=True) + EPS)
    spread(t_bot, send_ref)


def sum_kernel(got_ref, out_ref):
    out_ref[...] = jnp.sum(got_ref[...].astype(F32), axis=0)


def chunks(total, size):
    return [slice(j, j + size) for j in range(0, total, size)]


def expo_block(at, lhs_ref, rows_ref, e_ref):
    prod = lax.dot_general(lhs_ref[at, :], rows_ref[...], NT, preferred_element_type=F32)
    expo = jnp.exp(prod * (1.0 / teacher_temp))
    e_ref[at, :] = expo
    return jnp.sum(expo, axis=1, keepdims=True)


def teacher_own_kernel(w_ref, rows_ref, e_ref, lhs_ref, sums_ref):
    for at in chunks(w_ref.shape[1], CHUNK):
        lhs_ref[at, :] = columns(w_ref[:, at])[0].T.astype(BF16)
        sums_ref[at, :] = expo_block(at, lhs_ref, rows_ref, e_ref)


def teacher_other_kernel(total_cols, expected, lhs_ref, rows_ref, e_own, sums_ref, s_ref, e_ref, out_ref, acc):
    half = rows_ref.shape[0]
    acc[...] = jnp.zeros_like(acc)
    for at in chunks(lhs_ref.shape[0], CHUNK):
        scale = 1.0 / (total_cols * (sums_ref[at, :] + expo_block(at, lhs_ref, rows_ref, e_ref)))
        row_pass(e_own.at[at, :], scale, acc.at[:, :half])
        row_pass(e_ref.at[at, :], scale, acc.at[:, half:])
    sums = fold(jnp.sum(acc[...], axis=0, keepdims=True)) - expected
    spread(jnp.concatenate([sums, s_ref[...].astype(F32)], axis=0), out_ref)


def open_kernel(got_ref, sums_ref, rows_ref):
    total = jnp.zeros(sums_ref.shape, F32)
    for i in range(got_ref.shape[0]):
        piece = got_ref[i].astype(F32)
        total = total + piece[0:8, :]
        rows_ref[i] = piece[8:, :].astype(BF16)
    sums_ref[...] = total


def fold_half(part):
    row = jnp.sum(part, axis=0, keepdims=True)
    width = row.shape[1] // 4
    return jnp.concatenate([row[:, j * width : (j + 1) * width] for j in range(4)], axis=0)


def student_columns_kernel(w_ref, lhs_ref, cols_ref):
    for at in chunks(w_ref.shape[1], CHUNK):
        unit = columns(w_ref[:, at])[0]
        cols_ref[:, at] = unit.astype(BF16)
        lhs_ref[at, :] = unit.T.astype(BF16)


def student_kernel(start, lhs_ref, rows_ref, lg_ref, out_ref, part):
    part[...] = jnp.zeros_like(part)
    for at in chunks(lg_ref.shape[0], CHUNK):
        lhs = lhs_ref[start + at.start : start + at.stop, :]
        prod = lax.dot_general(lhs, rows_ref[...], NT, preferred_element_type=F32)
        logits = prod * (1.0 / student_temp)
        lg_ref[at, :] = logits
        part[...] += jnp.sum(jnp.exp(logits).reshape(CHUNK // 8, 8, logits.shape[1]), axis=0)
    out_ref[...] = fold_half(part[...])


def pair_kernel(row_ref, part_ref, out_ref):
    out_ref[...] = jnp.concatenate([row_ref[4:8, :], part_ref[...]], axis=0)


def send_kernel(row_ref, part_a, part_b, theirs_ref, out_ref):
    spread(jnp.concatenate([row_ref[0:4, :], part_a[...] + part_b[...]], axis=0) + theirs_ref[...], out_ref)


def pick(refs, at):
    if len(refs) == 1:
        return refs[0], at
    first = refs[0].shape[0]
    if at.stop <= first:
        return refs[0], at
    return refs[1], slice(at.start - first, at.stop - first)


def turn_kernel(rows_ref, out_ref):
    out_ref[...] = rows_ref[...].T


def row_pass(block_ref, scale, acc):
    rows, n = block_ref.shape
    scale = scale.reshape(rows // 8, 8, 1)
    for start in range(0, n, 512):
        lanes = slice(start, start + 512)
        acc[:, lanes] += jnp.sum(block_ref[:, lanes].reshape(rows // 8, 8, 512) * scale, axis=0)


def pass_kernel(total_cols, images, devices, own_ref, other_ref, mine_ref, theirs_ref, *rest):
    *before, out_ref, total_ref, cs_ref, weight, acc = rest
    total = total_row(mine_ref[...], theirs_ref[...])
    total = total + (flat(before[0][...]) if before else 1.0 / images)
    total_ref[...] = fold(total)
    weight[...] = jnp.broadcast_to(1.0 / (images * total), weight.shape)
    acc[...] = jnp.zeros_like(acc)
    protos, half = own_ref.shape

    def step(j, _):
        at = pl.ds(pl.multiple_of(j * BLOCK, BLOCK), BLOCK)
        sums = jnp.zeros((BLOCK, 1), F32)
        for ref, start in ((own_ref, 0), (other_ref, half)):
            weighted = ref[at, :].reshape(BLOCK // 8, 8, half) * weight[:, start : start + half][None]
            sums = sums + jnp.sum(weighted.reshape(BLOCK, half), axis=1, keepdims=True)
        scale = 1.0 / (total_cols * sums)
        cs_ref[at, :] = scale
        row_pass(own_ref.at[at, :], scale, acc.at[:, :half])
        row_pass(other_ref.at[at, :], scale, acc.at[:, half:])
        return 0

    lax.fori_loop(0, protos // BLOCK, step, 0)
    piece = fold(jnp.sum(acc[...], axis=0, keepdims=True)) - total_ref[...] * (1.0 / devices)
    if len(out_ref.shape) == 3:
        spread(piece, out_ref)
    else:
        out_ref[...] = piece


STRIP = 32
DEPTH = 512


def half_gradients(
    row, part, e_ref, lg_ref, cs_ref, cols_ref, turned_ref, db_ref, unit_sum, start, g, rows, cross, last=None
):
    protos, half = e_ref.shape
    rows[0:8, :] = jnp.broadcast_to((1.0 / student_temp) / part, (8, half))
    rows[8:16, :] = jnp.broadcast_to((1.0 / student_temp) / row, (8, half))
    folded = (STRIP // 8, 8, CHUNK)
    for _, _, acc in cross:
        acc[...] = jnp.zeros_like(acc)

    def elementwise(lanes):
        for at in chunks(protos, STRIP):
            for expo, logits, acc in cross:
                scaled = expo[at, lanes] * cs_ref[at, :]
                ref, place = pick(logits, at)
                acc[:, lanes] += jnp.sum((scaled * ref[place, lanes]).reshape(folded), axis=0)
            ref, place = pick(lg_ref, at)
            logits = ref[place, lanes]
            scaled = e_ref[at, lanes] * cs_ref[at, :]
            powers = jnp.exp(logits).reshape(folded) * rows[0:8, lanes][None]
            target = scaled.reshape(folded) * rows[8:16, lanes][None]
            g[at, lanes] = (powers - target).reshape(logits.shape).astype(BF16)

    def matmuls(lanes):
        db_ref[lanes, :] = jnp.dot(cols_ref[...], g[:, lanes], preferred_element_type=F32).T
        if lanes.stop % DEPTH == 0:
            deep = slice(lanes.stop - DEPTH, lanes.stop)
            if last is not None and lanes.stop == half:
                for at in chunks(protos, CHUNK):
                    term = lax.dot_general(turned_ref[:, deep], g[at, deep], NT, preferred_element_type=F32)
                    last(at, unit_sum[:, at] + term)
                return
            term = lax.dot_general(turned_ref[:, deep], g[:, deep], NT, preferred_element_type=F32)
            if lanes.stop > DEPTH:
                unit_sum[...] += term
            else:
                unit_sum[...] = term if start is None else start[...] + term

    before = None
    for lanes in chunks(half, CHUNK):
        elementwise(lanes)
        if before is not None:
            matmuls(before)
        before = lanes
    matmuls(before)


def grad_other_kernel(
    devices, e_ref, lg_other, cs_ref, cols_ref, turned_ref, mine_ref, theirs_ref, base_ref, e_own, lg_own_a, lg_own_b,
    db_ref, unit_sum, loss_ref, g, rows, acc, acc_own
):
    row = flat(theirs_ref[0:4, :] + base_ref[4:8, :])
    part = flat(theirs_ref[4:8, :])
    lg_ref = (lg_other,)
    cross = ((e_ref, lg_ref, acc), (e_own, (lg_own_a, lg_own_b), acc_own))
    half_gradients(row, part, e_ref, lg_ref, cs_ref, cols_ref, turned_ref, db_ref, unit_sum, None, g, rows, cross)
    parts = jnp.log(part) + jnp.log(flat(mine_ref[4:8, :]))
    row_own = flat(mine_ref[0:4, :] + base_ref[0:4, :])
    crossed = jnp.sum(acc[...], axis=0, keepdims=True) / row + jnp.sum(acc_own[...], axis=0, keepdims=True) / row_own
    terms = parts * (1.0 / devices) - crossed
    loss_ref[...] = sum(terms[:, lanes] for lanes in chunks(terms.shape[1], loss_ref.shape[1]))
    db_ref[e_ref.shape[1] :, :] = jnp.broadcast_to(loss_ref[...], (8, loss_ref.shape[1]))


def grad_own_kernel(
    e_ref, lg_a, lg_b, cs_ref, cols_ref, turned_ref, mine_ref, base_ref, other_sum, w_ref,
    db_ref, dp_ref, g, rows, unit_sum, out_buf, sem
):
    row = flat(mine_ref[0:4, :] + base_ref[0:4, :])
    part = flat(mine_ref[4:8, :])
    lg_ref = (lg_a, lg_b)
    copies = []

    def project(at, d_unit):
        unit, inv = columns(w_ref[:, at])
        out_buf[:, at] = inv * (d_unit - unit * jnp.sum(unit * d_unit, axis=0, keepdims=True))
        j = len(copies)
        copies.append(pltpu.make_async_copy(out_buf.at[:, at], dp_ref.at[:, at], sem.at[j]))
        copies[j].start()

    half_gradients(
        row, part, e_ref, lg_ref, cs_ref, cols_ref, turned_ref, db_ref, unit_sum, other_sum, g, rows, (), project
    )
    for copy in copies:
        copy.wait()


def parts_of(value):
    high = value.astype(BF16).astype(F32)
    mid = (value - high).astype(BF16).astype(F32)
    return high, mid, value - high - mid


def pack_kernel(mine_ref, theirs_ref, loss_ref, s_ref, out_ref):
    rows = mine_ref.shape[0]
    lane = lax.broadcasted_iota(jnp.int32, (8, 128), 1)
    total = jnp.sum(loss_ref[...] + theirs_ref[rows : rows + 1, :], axis=1, keepdims=True)
    loss = jnp.zeros((8, 128), F32)
    for j, part in enumerate(parts_of(total)):
        loss = jnp.where(lane == 9 + j, part, loss)

    group = 8

    def step(i, _):
        at = pl.ds(pl.multiple_of(i * 24 * group, 8), 24 * group)
        block = mine_ref[at, :] + theirs_ref[at, :]
        unit = s_ref[pl.ds(i * group, group)].astype(F32).reshape(block.shape)
        along = jnp.sum(block * unit, axis=1, keepdims=True)
        block = (block - unit * along).astype(BF16).reshape(group, 24, block.shape[1])
        parts = [part.reshape(group, 24, 1) for part in parts_of(along)]
        tail = jnp.broadcast_to(loss[None], (group, 8, 128))
        for j, part in enumerate(parts):
            for k in range(3):
                tail = jnp.where((lane == 3 * j + k)[None], part[:, 8 * k : 8 * (k + 1), :], tail)
        chips = pl.ds(i * group, group)
        for k in range(3):
            out_ref[chips, 24 * k : 24 * (k + 1), :] = block[:, :, 128 * k : 128 * (k + 1)]
        out_ref[chips, 72:80, :] = tail.astype(BF16)
        return 0

    lax.fori_loop(0, out_ref.shape[0] // group, step, 0, unroll=2)


def finish_kernel(images, got_ref, hid_ref, ds_ref, loss_ref):
    total = jnp.sum(got_ref[...].astype(F32), axis=0)
    tail = total[72:80, :]
    along = jnp.concatenate([tail[:, k : k + 1] + tail[:, 3 + k : 4 + k] + tail[:, 6 + k : 7 + k] for k in range(3)], axis=0)
    wide = hid_ref[...].astype(F32)
    inv = lax.rsqrt(jnp.sum(wide * wide, axis=1, keepdims=True) + EPS)
    unit = wide * inv
    d_bot = jnp.concatenate([total[24 * k : 24 * (k + 1), :] for k in range(3)], axis=1)
    d_bot = d_bot + unit.astype(BF16).astype(F32) * along
    ds_ref[...] = inv * (d_bot - unit * jnp.sum(unit * d_bot, axis=1, keepdims=True))
    loss = tail[0:1, 9:10] + tail[0:1, 10:11] + tail[0:1, 11:12]
    loss_ref[...] = jnp.broadcast_to(loss * (1.0 / images), loss_ref.shape)


def body(teacher_hidden, teacher_proj, student_hidden, teacher_protos, student_protos):
    chips = lax.axis_size(CHIPS)
    rows_dev, bot = student_hidden.shape
    half = rows_dev * chips
    images = 2 * half
    protos = teacher_protos.shape[1]
    total_cols = protos * lax.axis_size(ALL)
    sds = jax.ShapeDtypeStruct

    def swap(x):
        return lax.ppermute(x, "c", SWAP)

    def exchange(x):
        return lax.all_to_all(x, CHIPS, 0, 0)

    def row_sums(x, rows):
        mine = call(sum_kernel, sds((rows, images // 8), F32), (exchange(x),), 2)
        return mine, swap(mine)

    t_send, s_bot = call(
        rows_kernel,
        (sds((chips, rows_dev, bot), BF16), sds((rows_dev, bot), BF16)),
        (student_hidden, teacher_hidden, teacher_proj),
        60,
        [
            pltpu.VMEM(student_hidden.shape, BF16),
            pltpu.VMEM(teacher_hidden.shape, BF16),
            pltpu.VMEM((2, teacher_proj.shape[0] // 2, bot), BF16),
            pltpu.SemaphoreType.DMA((4,)),
        ],
        in_any=(0, 1, 2),
    )
    t_own = exchange(t_send).reshape(half, bot)
    t_other = swap(t_own)

    matrix = sds((protos, half), F32)
    lhs = sds((protos, bot), BF16)
    column = sds((protos, 1), F32)
    turned = sds((bot, half), BF16)
    vec8 = sds((8, images // 8), F32)
    vec4 = sds((4, images // 8), F32)
    send8 = sds((chips, 8, images // 8), BF16)
    fold8 = pltpu.VMEM((8, images), F32)
    half_acc = pltpu.VMEM((8, half), F32)
    scales = pltpu.VMEM((protos, 1), F32)

    e_own, t_lhs, sums = call(teacher_own_kernel, (matrix, lhs, column), (teacher_protos, t_own), 8)
    sums, student_late = lax.optimization_barrier((sums, student_protos))
    s_lhs, s_cols = call(student_columns_kernel, (lhs, sds((bot, protos), BF16)), (student_late,), 8)
    t_other, s_lhs, s_cols = lax.optimization_barrier((t_other, s_lhs, s_cols))
    e_other, sent = call(
        functools.partial(teacher_other_kernel, total_cols, 1.0 / (2 * chips * images)),
        (matrix, sds((chips, 8 + rows_dev, bot), BF16)),
        (t_lhs, t_other, e_own, sums, s_bot),
        8,
        [fold8],
    )
    mine, s_own = call(open_kernel, (vec8, sds((chips, rows_dev, bot), BF16)), (exchange(sent),), 4)
    theirs = swap(mine)
    s_own = s_own.reshape(half, bot)

    def student(start, stop, rows):
        shapes = (sds((stop - start, half), F32), vec4)
        return call(functools.partial(student_kernel, start), shapes, (s_lhs, rows), 8, [half_acc])

    split = protos // 2
    lg_own_a, part_own = student(0, split, s_own)
    theirs, part_own, s_late = lax.optimization_barrier((theirs, part_own, s_own))
    s_other = swap(s_late)
    one_pass = functools.partial(pass_kernel, total_cols, images, 2 * chips)
    sent, before = call(
        one_pass,
        (send8, vec8),
        (e_own, e_other, mine, theirs),
        4,
        [scales, fold8, fold8],
    )
    mine, theirs = row_sums(sent, 8)
    late, s_late = lax.optimization_barrier((mine, s_other))
    lg_other, part_other = student(0, protos, s_late)
    theirs, part_other = lax.optimization_barrier((theirs, part_other))
    row, before, col_scale = call(
        one_pass,
        (vec8, vec8, column),
        (e_own, e_other, late, theirs, before),
        4,
        [fold8, fold8],
    )
    pair_other = call(pair_kernel, vec8, (row, part_other), 2)
    pair_theirs = swap(pair_other)
    pair_other, own_late = lax.optimization_barrier((pair_other, s_own))
    lg_own_b, part_own_rest = student(split, protos, own_late)
    pair_theirs, part_own_rest = lax.optimization_barrier((pair_theirs, part_own_rest))
    mine, theirs = row_sums(call(send_kernel, send8, (row, part_own, part_own_rest, pair_theirs), 2), 8)
    mine, own_late, other_late = lax.optimization_barrier((mine, s_own, s_other))
    turned_own = call(turn_kernel, turned, (own_late,), 2)
    turned_other = call(turn_kernel, turned, (other_late,), 2)
    theirs, turned_own, turned_other = lax.optimization_barrier((theirs, turned_own, turned_other))
    tile = sds((1, bot), F32)
    grads = [pltpu.VMEM((protos, half), BF16), pltpu.VMEM((16, half), F32)]
    d_other, unit_sum, loss_mine = call(
        functools.partial(grad_other_kernel, 2 * chips),
        (sds((half + 8, bot), F32), sds((bot, protos), F32), tile),
        (e_other, lg_other, col_scale, s_cols, turned_other, mine, theirs, before, e_own, lg_own_a, lg_own_b),
        8,
        grads + [half_acc, half_acc],
    )
    d_theirs = swap(d_other)
    whole = pltpu.VMEM((bot, protos), F32)
    d_mine, d_protos = call(
        grad_own_kernel,
        (sds((half, bot), F32), sds((bot, protos), F32)),
        (e_own, lg_own_a, lg_own_b, col_scale, s_cols, turned_own, mine, before, unit_sum, student_protos),
        12,
        grads + [whole, whole, pltpu.SemaphoreType.DMA((protos // CHUNK,))],
        out_any=(1,),
    )
    packed = call(
        pack_kernel,
        sds((chips, 80, 128), BF16),
        (d_mine, d_theirs, loss_mine, s_own.reshape(chips, rows_dev, bot)),
        4,
    )
    got = exchange(packed)
    d_student, loss = call(
        functools.partial(finish_kernel, images),
        (sds((rows_dev, bot), F32), sds((1, 128), F32)),
        (got, student_hidden),
        4,
    )
    return loss[0, 0], d_student, d_protos


def solution(mesh):
    grid = Mesh(mesh.devices.reshape(4, 4, 4, 2), ALL)
    return jax.shard_map(
        body,
        mesh=grid,
        in_specs=(P(ALL, None), P(), P(ALL, None), P(None, ALL), P(None, ALL)),
        out_specs=(P(), P(ALL, None), P(None, ALL)),
        check_vma=False,
    )
```
